256 devices in a mesh: dp: 64 (over y_hi, z, x), tensor: 4 (over y_lo, core).
Axes of the slice: x: 4, y: 4 (y_hi: 2, y_lo: 2; y = y_hi * 2 + y_lo), z: 8, core: 2. Of those that a mesh axis runs over, the one named last changes fastest.
Arguments:
- hidden: bfloat16 [8192, 28672], P('dp', 'tensor'), may hold values from -6 to 6
- sign_bits: int32 [28672], P('tensor'), may hold values from 0 to 1
- exponents: int32 [8192, 224], P('dp', 'tensor'), may hold values from -9 to -6
- down_weight: bfloat16 [28672, 512], P('tensor'), may hold values from -0.03125 to 0.03125
- grad_out: bfloat16 [8192, 512], P('dp'), may hold values from -18 to 18
Outputs:
- output: bfloat16 [8192, 512], P(('dp', 'tensor'))
- grad_hidden: bfloat16 [8192, 28672], P('dp', 'tensor')
- grad_weight: float32 [28672, 512], P(('tensor', 'dp'))
The draws below stay inside these ranges and needn't reach their ends.
All inputs are finite; a program needn't handle non-finite values.
Results may differ from the reference program's by a relative error of at most 0.018.
Values may be sent and summed in bfloat16 or wider, within the bound.
No kernel may reach another device: no remote copies, remote signals or barrier semaphores. Data moves between devices by JAX's collectives and lax.ppermute only.
A program may use at most 192 MiB of HBM per device.

```python
import math
import jax
import jax.numpy as jnp
import numpy as np
from jax import lax

HB = 1024
FF = 28672
D_OUT = 512
GROUP = 128
TOKENS = 8192


def place_ends(values, rng, least, top_value):
    shape = values.shape
    place = [jax.random.randint(jax.random.fold_in(rng, axis), (), 0, shape[axis]) for axis in range(len(shape))]
    values = values.at[tuple(place)].set(least)
    longest = shape.index(max(shape))
    place[longest] = (place[longest] + 1) % shape[longest]
    return values.at[tuple(place)].set(top_value)


def level_of(rng, dims, cuts, smallest, top_value):
    level, own = 1.0, jax.random.fold_in(rng, 6)
    for axis_at, blocks in cuts:
        steps = jnp.exp(jax.random.uniform(jax.random.fold_in(own, axis_at), (blocks,), jnp.float32, smallest / len(cuts), top_value / len(cuts)))
        level = level * jnp.repeat(steps, dims[axis_at] // blocks).reshape([-1 if axis == axis_at else 1 for axis in range(len(dims))])
    return level


def gaussian(key, dims, scale, most, shards=(), dtype=jnp.bfloat16):
    drawn = jax.random.normal(key, dims, jnp.float32) * scale
    if len(shards) > 0:
        drawn = level_of(key, dims, shards, -0.22, 0.18) * drawn
    return jnp.clip(drawn, min=-most, max=most).astype(dtype)


def setup_inputs(seed: int = 0) -> dict:
    streams_of = jax.random.split(jax.random.key(seed), 6)
    hidden = gaussian(streams_of[0], (TOKENS, FF), 1.0, 6.0, ((0, 64), (1, 4)))
    sign_bits = place_ends(jax.random.randint(streams_of[1], (FF,), 0, 2), jax.random.fold_in(streams_of[1], 1), 0, 1).astype(jnp.int32)
    exponents = place_ends(jax.random.randint(streams_of[2], (TOKENS, FF // GROUP), -9, -5), jax.random.fold_in(streams_of[2], 1), -9, (-5) - 1).astype(jnp.int32)
    down_weight = gaussian(streams_of[3], (FF, D_OUT), FF ** -0.5, 0.03125, ((0, 4),))
    grad_out = gaussian(streams_of[4], (TOKENS, D_OUT), 3.0, 18.0, ((0, 64),))
    return {"hidden": hidden, "sign_bits": sign_bits, "exponents": exponents, "down_weight": down_weight, "grad_out": grad_out}


def paley_table():
    squares_set = set((factor * factor % 13 for factor in range(1, 13)))
    core_matrix = np.zeros((14, 14))
    core_matrix[0, 1:] = 1.0
    core_matrix[1:, 0] = 1.0
    for row_idx in range(13):
        for col_idx in range(13):
            offset = (col_idx - row_idx) % 13
            if offset != 0:
                core_matrix[row_idx + 1, col_idx + 1] = 1.0 if offset in squares_set else -1.0
    first_pat = np.array([[1.0, -1.0], [-1.0, -1.0]])
    second_pat = np.array([[1.0, 1.0], [1.0, -1.0]])
    return np.kron(core_matrix, first_pat) + np.kron(np.eye(14), second_pat)

def sylvester_table(order):
    result = np.ones((1, 1))
    base_pat = np.array([[1.0, 1.0], [1.0, -1.0]])
    while result.shape[0] < order:
        result = np.kron(base_pat, result)
    return result

def spin_all(values):
    tok_rows = values.shape[0]
    cube = values.reshape(tok_rows, HB, 28)
    cube = jnp.einsum('tba,cb->tca', cube, jnp.asarray(sylvester_table(HB), jnp.float32), precision=lax.Precision.HIGHEST)
    cube = jnp.einsum('tca,da->tcd', cube, jnp.asarray(paley_table(), jnp.float32), precision=lax.Precision.HIGHEST)
    return cube.reshape(tok_rows, FF) / math.sqrt(FF)

def reference(hidden, sign_bits, exponents, down_weight, grad_out):
    sign_vals = (2 * sign_bits - 1).astype(jnp.float32)
    block_rows = math.gcd(TOKENS, 512)
    count_blocks = TOKENS // block_rows

    def per_block(inputs):
        hid_block, expo_block, grad_block = inputs
        rotated = spin_all(hid_block.astype(jnp.float32) * sign_vals[None, :])
        bound = 448.0 * jnp.exp2(expo_block.astype(jnp.float32))[:, :, None]
        ratio = jnp.tanh(rotated.reshape(block_rows, FF // GROUP, GROUP) / bound)
        quantized = (bound * ratio).reshape(block_rows, FF).astype(jnp.bfloat16)
        output = jnp.dot(quantized, down_weight, preferred_element_type=jnp.float32).astype(jnp.bfloat16)
        grad_quant = lax.dot_general(grad_block, down_weight, (((1,), (1,)), ((), ())), preferred_element_type=jnp.float32)
        grad_rot = grad_quant * (1.0 - ratio * ratio).reshape(block_rows, FF)
        grad_hidden = (spin_all(grad_rot) * sign_vals[None, :]).astype(jnp.bfloat16)
        return (output, grad_hidden, quantized)
    results_all = lax.map(per_block, (hidden.reshape(count_blocks, block_rows, FF), exponents.reshape(count_blocks, block_rows, FF // GROUP), grad_out.reshape(count_blocks, block_rows, D_OUT)))
    output = results_all[0].reshape(TOKENS, D_OUT)
    grad_hidden = results_all[1].reshape(TOKENS, FF)
    quantized_all = results_all[2].reshape(TOKENS, FF)
    grad_weight = lax.dot_general(quantized_all, grad_out, (((0,), (0,)), ((), ())), preferred_element_type=jnp.float32) * (1.0 / math.sqrt(TOKENS))
    return (output, grad_hidden, grad_weight)
```

```python
import functools
import math

import jax
import jax.numpy as jnp
import numpy as np
from jax import lax
from jax.experimental import pallas as pl
from jax.experimental.pallas import tpu as pltpu
from jax.sharding import Mesh
from jax.sharding import PartitionSpec as P

AXES = ("yh", "z", "x", "yl", "core")
BLOCK = 896
LANES = 128


def paley_table():
    squares_set = set((factor * factor % 13 for factor in range(1, 13)))
    core_matrix = np.zeros((14, 14))
    core_matrix[0, 1:] = 1.0
    core_matrix[1:, 0] = 1.0
    for row_idx in range(13):
        for col_idx in range(13):
            offset = (col_idx - row_idx) % 13
            if offset != 0:
                core_matrix[row_idx + 1, col_idx + 1] = 1.0 if offset in squares_set else -1.0
    first_pat = np.array([[1.0, -1.0], [-1.0, -1.0]])
    second_pat = np.array([[1.0, 1.0], [1.0, -1.0]])
    return np.kron(core_matrix, first_pat) + np.kron(np.eye(14), second_pat)


def sylvester_table(order):
    result = np.ones((1, 1))
    base_pat = np.array([[1.0, 1.0], [1.0, -1.0]])
    while result.shape[0] < order:
        result = np.kron(base_pat, result)
    return result


def block_table():
    return np.kron(sylvester_table(BLOCK // 28), paley_table())


def pairs_xor():
    return [(0, 1), (1, 0)]


def swap(value, axis):
    return lax.ppermute(value, axis, pairs_xor())


def butterfly(parts):
    parts = list(parts)
    step = 1
    while step < len(parts):
        for base in range(len(parts)):
            if base & step == 0:
                a, b = parts[base], parts[base + step]
                parts[base], parts[base + step] = a + b, a - b
        step *= 2
    return parts


def rotate_kernel(nblk, norm, sgn_ref, own_ref, core_ref, far_ref, fcore_ref, table_ref, bound_ref, q_ref, slope_ref, qt_ref, w_ref, spun_ref):
    rows = own_ref.shape[0]
    so_core, so_y = sgn_ref[0], sgn_ref[1]
    for j in range(nblk):
        cols = pl.ds(j * BLOCK, BLOCK)
        near = so_core * own_ref[:, cols].astype(jnp.float32) + core_ref[:, cols].astype(jnp.float32)
        far = so_core * far_ref[:, cols].astype(jnp.float32) + fcore_ref[:, cols].astype(jnp.float32)
        w_ref[pl.ds(j * rows, rows), :] = (so_y * near + far).astype(jnp.bfloat16)
    spun_ref[...] = jnp.dot(w_ref[...], table_ref[...], preferred_element_type=jnp.float32)
    half = nblk // 2
    for lane in range(BLOCK // LANES):
        lcols = pl.ds(lane * LANES, LANES)
        parts = butterfly([spun_ref[pl.ds(j * rows, rows), lcols] for j in range(nblk)])
        quants = []
        for j in range(nblk):
            group = j * (BLOCK // LANES) + lane
            bound = bound_ref[:, group : group + 1]
            ratio = jnp.tanh(parts[j] * (norm / bound))
            quant = bound * ratio
            cols = pl.ds(j * BLOCK + lane * LANES, LANES)
            q_ref[:, cols] = quant.astype(jnp.bfloat16)
            slope_ref[:, cols] = (1.0 - ratio * ratio).astype(jnp.bfloat16)
            quants.append(quant)
        for j in range(half):
            both = jnp.concatenate([quants[j], quants[j + half]], axis=0)
            qt_ref[pl.ds(j * BLOCK + lane * LANES, LANES), :] = both.T.astype(jnp.bfloat16)


def rotate(sgn, own, core, far, fcore, table, bound, norm):
    rows, cols = own.shape
    nblk = cols // BLOCK
    vm = pl.BlockSpec(memory_space=pltpu.VMEM)
    return pl.pallas_call(
        functools.partial(rotate_kernel, nblk, norm),
        out_shape=(
            jax.ShapeDtypeStruct((rows, cols), jnp.bfloat16),
            jax.ShapeDtypeStruct((rows, cols), jnp.bfloat16),
            jax.ShapeDtypeStruct((cols // 2, 2 * rows), jnp.bfloat16),
        ),
        in_specs=[pl.BlockSpec(memory_space=pltpu.SMEM)] + [vm] * 6,
        out_specs=(vm, vm, vm),
        scratch_shapes=[
            pltpu.VMEM((nblk * rows, BLOCK), jnp.bfloat16),
            pltpu.VMEM((nblk * rows, BLOCK), jnp.float32),
        ],
        compiler_params=pltpu.CompilerParams(vmem_limit_bytes=40 * 2**20),
        name="rotate",
    )(sgn, own, core, far, fcore, table, bound)


def project_kernel(nblk, norm, q_ref, slope_ref, go_ref, w_ref, table_ref, out_ref, s_ref, acc_ref, g_ref, spun_ref):
    j = pl.program_id(0)
    rows = q_ref.shape[0]
    weight = w_ref[...]
    part = jnp.dot(q_ref[...], weight, preferred_element_type=jnp.float32)

    @pl.when(j == 0)
    def _():
        acc_ref[...] = part

    @pl.when(j > 0)
    def _():
        acc_ref[...] += part

    grad = lax.dot_general(go_ref[...], weight, (((1,), (1,)), ((), ())), preferred_element_type=jnp.float32)
    start = pl.multiple_of(j * rows, rows)
    g_ref[pl.ds(start, rows), :] = (grad * slope_ref[...].astype(jnp.float32)).astype(jnp.bfloat16)

    @pl.when(j == nblk - 1)
    def _():
        out_ref[...] = acc_ref[...].astype(out_ref.dtype)
        spun_ref[...] = jnp.dot(g_ref[...], table_ref[...], preferred_element_type=jnp.float32)
        for lane in range(BLOCK // LANES):
            lcols = pl.ds(lane * LANES, LANES)
            parts = butterfly([spun_ref[pl.ds(b * rows, rows), lcols] for b in range(nblk)])
            for b in range(nblk):
                s_ref[:, pl.ds(b * BLOCK + lane * LANES, LANES)] = (parts[b] * norm).astype(jnp.bfloat16)


def project(quant, slope, grad_out, weight, table, norm):
    rows, cols = quant.shape
    nblk = cols // BLOCK
    wide = weight.shape[1]
    return pl.pallas_call(
        functools.partial(project_kernel, nblk, norm),
        grid=(nblk,),
        out_shape=(
            jax.ShapeDtypeStruct((rows, wide), jnp.bfloat16),
            jax.ShapeDtypeStruct((rows, cols), jnp.bfloat16),
        ),
        in_specs=[
            pl.BlockSpec((rows, BLOCK), lambda j: (0, j)),
            pl.BlockSpec((rows, BLOCK), lambda j: (0, j)),
            pl.BlockSpec((rows, wide), lambda j: (0, 0)),
            pl.BlockSpec((BLOCK, wide), lambda j: (j, 0)),
            pl.BlockSpec((BLOCK, BLOCK), lambda j: (0, 0)),
        ],
        out_specs=(
            pl.BlockSpec((rows, wide), lambda j: (0, 0)),
            pl.BlockSpec((rows, cols), lambda j: (0, 0)),
        ),
        scratch_shapes=[
            pltpu.VMEM((rows, wide), jnp.float32),
            pltpu.VMEM((nblk * rows, BLOCK), jnp.bfloat16),
            pltpu.VMEM((nblk * rows, BLOCK), jnp.float32),
        ],
        compiler_params=pltpu.CompilerParams(vmem_limit_bytes=40 * 2**20),
        name="project",
    )(quant, slope, grad_out, weight, table)


def weight_grad_kernel(nsrc, rows, r_ref, go_ref, acc_in_ref, out_ref, lhs_ref, rhs_ref):
    toks = LANES // 2
    lane = lax.broadcasted_iota(jnp.int32, (rows, LANES), 1)
    low = lane < toks
    for s in range(nsrc):
        value = r_ref[s]
        zero = jnp.zeros_like(value)
        cols = pl.ds(s * LANES, LANES)
        lhs_ref[0:rows, cols] = jnp.where(low, value, zero)
        lhs_ref[rows : 2 * rows, cols] = jnp.where(low, zero, value)
        grads = go_ref[s]
        rhs_ref[pl.ds(s * LANES, toks), :] = grads
        rhs_ref[pl.ds(s * LANES + toks, toks), :] = grads
    out_ref[...] = acc_in_ref[...] + jnp.dot(lhs_ref[...], rhs_ref[...], preferred_element_type=jnp.float32)


def weight_grad(received, grads, chunk, acc):
    nsrc, rows, _ = received.shape
    toks, wide = LANES // 2, grads.shape[2]
    return pl.pallas_call(
        functools.partial(weight_grad_kernel, nsrc, rows),
        grid=(1,),
        out_shape=jax.ShapeDtypeStruct((2 * rows, wide), jnp.float32),
        in_specs=[
            pl.BlockSpec((nsrc, rows, LANES), lambda i: (0, 0, 0)),
            pl.BlockSpec((nsrc, toks, wide), lambda i: (0, chunk, 0)),
            pl.BlockSpec((2 * rows, wide), lambda i: (0, 0)),
        ],
        out_specs=pl.BlockSpec((2 * rows, wide), lambda i: (0, 0)),
        scratch_shapes=[
            pltpu.VMEM((2 * rows, nsrc * LANES), jnp.bfloat16),
            pltpu.VMEM((nsrc * LANES, wide), jnp.bfloat16),
        ],
        compiler_params=pltpu.CompilerParams(vmem_limit_bytes=48 * 2**20),
        name="weight_grad",
    )(received, grads, acc)


def gather_zx(value):
    return lax.all_gather(value, ("z", "x"), axis=0, tiled=False)


def exchange_zx(quant_t):
    nsrc = lax.axis_size("z") * lax.axis_size("x")
    blocks = quant_t.reshape(nsrc, -1, quant_t.shape[1])
    return lax.all_to_all(blocks, ("z", "x"), 0, 0, tiled=True)


def local(hidden, sign_bits, exponents, down_weight, grad_out):
    tok_count, ff_local = hidden.shape
    n_tensor = lax.axis_size("yl") * lax.axis_size("core")
    n_data = lax.axis_size("yh") * lax.axis_size("z") * lax.axis_size("x")
    norm = 1.0 / math.sqrt(ff_local * n_tensor)
    half = tok_count // 2
    table = jnp.asarray(block_table(), jnp.bfloat16)
    sign_vals = (2 * sign_bits - 1).astype(jnp.bfloat16)[None, :]
    core, yl, yh = lax.axis_index("core"), lax.axis_index("yl"), lax.axis_index("yh")
    so_core = (1 - 2 * core).astype(jnp.float32)
    so_y = (1 - 2 * yl).astype(jnp.float32)
    sgn = jnp.stack([so_core, so_y])
    bound = 448.0 * jnp.exp2(exponents.astype(jnp.float32))

    flipped = [hidden[k * half : (k + 1) * half] * sign_vals for k in range(2)]
    far = [swap(f, "yl") for f in flipped]
    near = [swap(f, "core") for f in flipped]
    grads_all = gather_zx(grad_out)

    outs, folded, crossed, received = [], [], [], []
    for k in range(2):
        rows = slice(k * half, (k + 1) * half)
        fcore = swap(far[k], "core")
        quant, slope, quant_t = rotate(sgn, flipped[k], near[k], far[k], fcore, table, bound[rows], norm)
        out, spun = project(quant, slope, grad_out[rows], down_weight, table, norm)
        outs.append(out)
        partner = swap(spun, "core")
        fold = (so_core * spun.astype(jnp.float32) + partner.astype(jnp.float32)).astype(jnp.bfloat16)
        folded.append(fold)
        crossed.append(swap(fold, "yl"))
        received.append(exchange_zx(quant_t))

    out_all = jnp.concatenate(outs, axis=0).reshape(2, 2, -1, outs[0].shape[1])
    keep = lax.dynamic_index_in_dim(out_all, yl, 0, keepdims=False)
    give = lax.dynamic_index_in_dim(out_all, 1 - yl, 0, keepdims=False)
    summed = keep.astype(jnp.float32) + swap(give, "yl").astype(jnp.float32)
    keep = lax.dynamic_index_in_dim(summed, core, 0, keepdims=False)
    give = lax.dynamic_index_in_dim(summed, 1 - core, 0, keepdims=False).astype(jnp.bfloat16)
    output = (keep + swap(give, "core").astype(jnp.float32)).astype(jnp.bfloat16)

    acc = jnp.zeros((2 * received[0].shape[1], grad_out.shape[1]), jnp.float32)
    for k in range(2):
        acc = weight_grad(received[k], grads_all, k, acc)
    acc = acc.reshape(2, -1, grad_out.shape[1])
    mine = lax.dynamic_index_in_dim(acc, yh, 0, keepdims=False)
    give = lax.dynamic_index_in_dim(acc, 1 - yh, 0, keepdims=False).astype(jnp.bfloat16)
    inv_root = 1.0 / math.sqrt(tok_count * n_data)
    grad_weight = (mine + swap(give, "yh").astype(jnp.float32)) * inv_root

    grad_hidden = jnp.concatenate(
        [
            (so_y * folded[k].astype(jnp.float32) + crossed[k].astype(jnp.float32)).astype(jnp.bfloat16) * sign_vals
            for k in range(2)
        ],
        axis=0,
    )
    return (output, grad_hidden, grad_weight)


def solution(mesh):
    fine = Mesh(mesh.devices.reshape(2, 8, 4, 2, 2), AXES)
    dp, tensor = ("yh", "z", "x"), ("yl", "core")
    return jax.shard_map(
        local,
        mesh=fine,
        in_specs=(P(dp, tensor), P(tensor), P(dp, tensor), P(tensor, None), P(dp, None)),
        out_specs=(P(dp + tensor, None), P(dp, tensor), P(tensor + dp, None)),
        check_vma=False,
    )
```

```python
import functools
import math

import jax
import jax.numpy as jnp
import numpy as np
from jax import lax
from jax.experimental import pallas as pl
from jax.experimental.pallas import tpu as pltpu
from jax.sharding import Mesh
from jax.sharding import PartitionSpec as P

AXES = ("yh", "z", "x", "yl", "core")
BLOCK = 896
LANES = 128
VM = pl.BlockSpec(memory_space=pltpu.VMEM)
SM = pl.BlockSpec(memory_space=pltpu.SMEM)
ANY = pl.BlockSpec(memory_space=pl.ANY)


def paley_table():
    squares_set = set((factor * factor % 13 for factor in range(1, 13)))
    core_matrix = np.zeros((14, 14))
    core_matrix[0, 1:] = 1.0
    core_matrix[1:, 0] = 1.0
    for row_idx in range(13):
        for col_idx in range(13):
            offset = (col_idx - row_idx) % 13
            if offset != 0:
                core_matrix[row_idx + 1, col_idx + 1] = 1.0 if offset in squares_set else -1.0
    first_pat = np.array([[1.0, -1.0], [-1.0, -1.0]])
    second_pat = np.array([[1.0, 1.0], [1.0, -1.0]])
    return np.kron(core_matrix, first_pat) + np.kron(np.eye(14), second_pat)


def sylvester_table(order):
    result = np.ones((1, 1))
    base_pat = np.array([[1.0, 1.0], [1.0, -1.0]])
    while result.shape[0] < order:
        result = np.kron(base_pat, result)
    return result


def block_table():
    return np.kron(sylvester_table(BLOCK // 28), paley_table())


def swap(value, axis):
    return lax.ppermute(value, axis, [(0, 1), (1, 0)])


def shift(value, axis, by):
    size = lax.axis_size(axis)
    return lax.ppermute(value, axis, [(i, (i + by) % size) for i in range(size)])


def params(mib):
    return pltpu.CompilerParams(vmem_limit_bytes=mib * 2**20)


def cost(flops, nbytes):
    return pl.CostEstimate(flops=flops, bytes_accessed=nbytes, transcendentals=0)


def butterfly(parts):
    parts = list(parts)
    step = 1
    while step < len(parts):
        for base in range(len(parts)):
            if base & step == 0:
                a, b = parts[base], parts[base + step]
                parts[base], parts[base + step] = a + b, a - b
        step *= 2
    return parts


def flip_kernel(h_ref, sign_ref, *rest):
    out_ref = rest[-1]
    sign = (2 * sign_ref[...] - 1).astype(jnp.float32)
    out_ref[...] = (h_ref[...].astype(jnp.float32) * sign).astype(jnp.bfloat16)


def flip(hidden, sign_bits, chunk, rows, after=()):
    cols = hidden.shape[1]
    wide = 2 * BLOCK
    return pl.pallas_call(
        flip_kernel,
        grid=(cols // wide,),
        out_shape=jax.ShapeDtypeStruct((rows, cols), jnp.bfloat16),
        in_specs=[
            pl.BlockSpec((rows, wide), lambda j: (chunk, j)),
            pl.BlockSpec((1, wide), lambda j: (0, j)),
        ]
        + [ANY] * len(after),
        out_specs=pl.BlockSpec((rows, wide), lambda j: (0, j)),
        compiler_params=params(16),
        cost_estimate=cost(rows * cols, 4 * rows * cols),
        name="flip",
    )(hidden, sign_bits, *after)


def fold_kernel(sgn_ref, a_ref, b_ref, *rest):
    out_ref = rest[-1]
    total = sgn_ref[0] * a_ref[...].astype(jnp.float32) + b_ref[...].astype(jnp.float32)
    out_ref[...] = total.astype(jnp.bfloat16)


def fold(sgn, a, b, after=()):
    rows, cols = a.shape
    wide = 2 * BLOCK
    block = pl.BlockSpec((rows, wide), lambda j: (0, j))
    return pl.pallas_call(
        fold_kernel,
        grid=(cols // wide,),
        out_shape=jax.ShapeDtypeStruct((rows, cols), jnp.bfloat16),
        in_specs=[SM, block, block] + [ANY] * len(after),
        out_specs=block,
        compiler_params=params(16),
        cost_estimate=cost(2 * rows * cols, 6 * rows * cols),
        name="fold",
    )(sgn, a, b, *after)


def finish_kernel(sgn_ref, a_ref, b_ref, sign_ref, *rest):
    out_ref = rest[-1]
    total = sgn_ref[0] * a_ref[...].astype(jnp.float32) + b_ref[...].astype(jnp.float32)
    sign = (2 * sign_ref[...] - 1).astype(jnp.float32)
    out_ref[...] = (total * sign).astype(jnp.bfloat16)


def finish(sgn, a, b, sign_bits, chunk, into=None):
    rows, cols = a.shape
    wide = 2 * BLOCK
    block = pl.BlockSpec((rows, wide), lambda j: (0, j))
    more = [] if into is None else [into]
    return pl.pallas_call(
        finish_kernel,
        grid=(cols // wide,),
        out_shape=jax.ShapeDtypeStruct((2 * rows, cols), jnp.bfloat16),
        in_specs=[SM, block, block, pl.BlockSpec((1, wide), lambda j: (0, j))] + [ANY] * len(more),
        out_specs=pl.BlockSpec((rows, wide), lambda j: (chunk, j)),
        input_output_aliases={4: 0} if more else {},
        compiler_params=params(16),
        cost_estimate=cost(2 * rows * cols, 6 * rows * cols),
        name="finish",
    )(sgn, a, b, sign_bits, *more)


def back_kernel(go_ref, w_ref, *rest):
    out_ref = rest[-1]
    grad = lax.dot_general(go_ref[...], w_ref[...], (((1,), (1,)), ((), ())), preferred_element_type=jnp.float32)
    out_ref[...] = grad.astype(out_ref.dtype)


def back(grad_out, weight, after=()):
    rows, wide = grad_out.shape
    cols = weight.shape[0]
    return pl.pallas_call(
        back_kernel,
        grid=(cols // BLOCK,),
        out_shape=jax.ShapeDtypeStruct((rows, cols), jnp.float32),
        in_specs=[
            pl.BlockSpec((rows, wide), lambda j: (0, 0)),
            pl.BlockSpec((BLOCK, wide), lambda j: (j, 0)),
        ]
        + [ANY] * len(after),
        out_specs=pl.BlockSpec((rows, BLOCK), lambda j: (0, j)),
        compiler_params=params(24),
        cost_estimate=cost(2 * rows * cols * wide, 2 * cols * wide + 4 * rows * cols),
        name="back",
    )(grad_out, weight, *after)


def project_kernel(q0_ref, q1_ref, w_ref, *rest):
    out_ref, acc_ref = rest[-2:]
    j = pl.program_id(0)
    quant = jnp.concatenate([q0_ref[...], q1_ref[...]], axis=0)
    part = jnp.dot(quant, w_ref[...], preferred_element_type=jnp.float32)

    @pl.when(j == 0)
    def _():
        acc_ref[...] = part

    @pl.when(j > 0)
    def _():
        acc_ref[...] += part

    @pl.when(j == pl.num_programs(0) - 1)
    def _():
        out_ref[...] = acc_ref[...].astype(out_ref.dtype)


def project(quants, weight, after=()):
    rows, cols = quants[0].shape
    wide = weight.shape[1]
    block = pl.BlockSpec((rows, BLOCK), lambda j: (0, j))
    return pl.pallas_call(
        project_kernel,
        grid=(cols // BLOCK,),
        out_shape=jax.ShapeDtypeStruct((2 * rows, wide), jnp.bfloat16),
        in_specs=[block, block, pl.BlockSpec((BLOCK, wide), lambda j: (j, 0))] + [ANY] * len(after),
        out_specs=pl.BlockSpec((2 * rows, wide), lambda j: (0, 0)),
        scratch_shapes=[pltpu.VMEM((2 * rows, wide), jnp.float32)],
        compiler_params=params(24),
        cost_estimate=cost(4 * rows * cols * wide, 2 * cols * wide),
        name="project",
    )(*quants, weight, *after)


def turn_kernel(nblk, norm, n_in, sgn_ref, *refs):
    ins, (table_ref, bound_ref, gq_ref), refs = refs[:n_in], refs[n_in : n_in + 3], refs[n_in + 3 :]
    q_ref, qt_ref, s_ref, w_ref, spun_ref = refs[-5:]
    rows = ins[0].shape[0]
    so_core, so_y = sgn_ref[0], sgn_ref[1]
    for j in range(nblk):
        cols = pl.ds(j * BLOCK, BLOCK)
        parts = [r[:, cols].astype(jnp.float32) for r in ins]
        if n_in == 4:
            parts = [so_core * parts[0] + parts[1], so_core * parts[2] + parts[3]]
        w_ref[pl.ds(j * rows, rows), :] = (so_y * parts[0] + parts[1]).astype(jnp.bfloat16)
    spun_ref[...] = jnp.dot(w_ref[...], table_ref[...], preferred_element_type=jnp.float32)
    half = nblk // 2
    for lane in range(BLOCK // LANES):
        lcols = pl.ds(lane * LANES, LANES)
        parts = butterfly([spun_ref[pl.ds(j * rows, rows), lcols] for j in range(nblk)])
        quants = []
        for j in range(nblk):
            group = j * (BLOCK // LANES) + lane
            bound = bound_ref[:, group : group + 1]
            ratio = jnp.tanh(parts[j] * (norm / bound))
            quant = bound * ratio
            cols = pl.ds(j * BLOCK + lane * LANES, LANES)
            q_ref[:, cols] = quant.astype(jnp.bfloat16)
            grad = gq_ref[:, cols] * (1.0 - ratio * ratio)
            w_ref[pl.ds(j * rows, rows), lcols] = grad.astype(jnp.bfloat16)
            quants.append(quant)
        for j in range(half):
            both = jnp.concatenate([quants[j], quants[j + half]], axis=0)
            qt_ref[pl.ds(j * BLOCK + lane * LANES, LANES), :] = both.T.astype(jnp.bfloat16)
    spun_ref[...] = jnp.dot(w_ref[...], table_ref[...], preferred_element_type=jnp.float32)
    for lane in range(BLOCK // LANES):
        lcols = pl.ds(lane * LANES, LANES)
        parts = butterfly([spun_ref[pl.ds(j * rows, rows), lcols] for j in range(nblk)])
        for j in range(nblk):
            s_ref[:, pl.ds(j * BLOCK + lane * LANES, LANES)] = (parts[j] * norm).astype(jnp.bfloat16)


def turn(sgn, ins, table, bound, gq, chunk, norm, after=()):
    rows, cols = ins[0].shape
    nblk = cols // BLOCK
    return pl.pallas_call(
        functools.partial(turn_kernel, nblk, norm, len(ins)),
        grid=(1,),
        out_shape=(
            jax.ShapeDtypeStruct((rows, cols), jnp.bfloat16),
            jax.ShapeDtypeStruct((cols // 2, 2 * rows), jnp.bfloat16),
            jax.ShapeDtypeStruct((rows, cols), jnp.bfloat16),
        ),
        in_specs=[SM]
        + [VM] * (len(ins) + 1)
        + [
            pl.BlockSpec((rows, bound.shape[1]), lambda i: (chunk, 0)),
            pl.BlockSpec((rows, cols), lambda i: (chunk, 0)),
        ]
        + [ANY] * len(after),
        out_specs=(VM, VM, VM),
        scratch_shapes=[
            pltpu.VMEM((nblk * rows, BLOCK), jnp.bfloat16),
            pltpu.VMEM((nblk * rows, BLOCK), jnp.float32),
        ],
        compiler_params=params(44),
        cost_estimate=cost(4 * rows * cols * BLOCK, 2 * rows * cols * (len(ins) + 5)),
        name="turn",
    )(sgn, *ins, table, bound, gq, *after)


def weight_grad_kernel(nsrc, rows, chunk, src_ref, r_ref, mine_ref, theirs_ref, acc_in_ref, out_ref, lhs_ref, rhs_ref):
    toks = LANES // 2
    low = lax.broadcasted_iota(jnp.int32, (rows, LANES), 1) < toks
    is_mine = src_ref[nsrc] == chunk
    for s in range(nsrc):
        value = r_ref[src_ref[s]]
        zero = jnp.zeros_like(value)
        cols = pl.ds(s * LANES, LANES)
        lhs_ref[0:rows, cols] = jnp.where(low, value, zero)
        lhs_ref[rows : 2 * rows, cols] = jnp.where(low, zero, value)
        here = pl.ds(s * toks, toks)
        grads = jnp.where(is_mine, mine_ref[here, :], theirs_ref[here, :])
        rhs_ref[pl.ds(s * LANES, toks), :] = grads
        rhs_ref[pl.ds(s * LANES + toks, toks), :] = grads
    out_ref[...] = acc_in_ref[...] + jnp.dot(lhs_ref[...], rhs_ref[...], preferred_element_type=jnp.float32)


def weight_grad(sources, received, mine, theirs, chunk, acc):
    nsrc, rows, _ = received.shape
    wide = mine.shape[1]
    return pl.pallas_call(
        functools.partial(weight_grad_kernel, nsrc, rows, chunk),
        grid=(1,),
        out_shape=jax.ShapeDtypeStruct((2 * rows, wide), jnp.float32),
        in_specs=[SM, VM, VM, VM, VM],
        out_specs=VM,
        scratch_shapes=[
            pltpu.VMEM((2 * rows, nsrc * LANES), jnp.bfloat16),
            pltpu.VMEM((nsrc * LANES, wide), jnp.bfloat16),
        ],
        compiler_params=params(40),
        cost_estimate=cost(8 * rows * nsrc * LANES * wide, 2 * nsrc * LANES * (rows + wide)),
        name="weight_grad",
    )(sources, received, mine, theirs, acc)


def gather_ring(value):
    nx, nz = lax.axis_size("x"), lax.axis_size("z")
    up, down = shift(value, "x", 1), shift(value, "x", nx - 1)
    far = shift(value, "x", 2)
    here = jnp.concatenate([value, up, far, down], axis=0)
    blocks = [None] * nz
    blocks[0] = here
    forth = back_ = here
    for step in range(1, nz // 2 + 1):
        forth = shift(forth, "z", 1)
        blocks[step] = forth
        if step < nz // 2:
            back_ = shift(back_, "z", nz - 1)
            blocks[nz - step] = back_
    return jnp.concatenate(blocks, axis=0)


def relative_sources():
    nx, nz = lax.axis_size("x"), lax.axis_size("z")
    z, x = lax.axis_index("z"), lax.axis_index("x")
    dz, dx = jnp.arange(nz)[:, None], jnp.arange(nx)[None, :]
    return (((z - dz) % nz) * nx + (x - dx) % nx).reshape(-1)


def exchange_zx(quant_t):
    nsrc = lax.axis_size("z") * lax.axis_size("x")
    blocks = quant_t.reshape(nsrc, -1, quant_t.shape[1])
    return lax.all_to_all(blocks, ("z", "x"), 0, 0, tiled=True)


def local(hidden, sign_bits, exponents, down_weight, grad_out):
    tok_count, ff_local = hidden.shape
    n_tensor = lax.axis_size("yl") * lax.axis_size("core")
    n_data = lax.axis_size("yh") * lax.axis_size("z") * lax.axis_size("x")
    norm = 1.0 / math.sqrt(ff_local * n_tensor)
    half = tok_count // 2
    table = jnp.asarray(block_table(), jnp.bfloat16)
    sign_bits = sign_bits.reshape(1, ff_local)
    core, yl, yh = lax.axis_index("core"), lax.axis_index("yl"), lax.axis_index("yh")
    so_core = (1 - 2 * core).astype(jnp.float32)
    so_y = (1 - 2 * yl).astype(jnp.float32)
    sgn_c, sgn_y, sgn = so_core[None], so_y[None], jnp.stack([so_core, so_y])
    bound = 448.0 * jnp.exp2(exponents.astype(jnp.float32))

    flip0 = flip(hidden, sign_bits, 0, half)
    far0 = swap(flip0, "yl")
    flip1 = flip(hidden, sign_bits, 1, half, after=(flip0,))
    near1 = swap(flip1, "core")
    near0 = swap(flip0, "core")
    both1 = fold(sgn_c, flip1, near1)
    far1 = swap(both1, "yl")
    gq = back(grad_out, down_weight, after=(both1,))

    mine = gather_ring(lax.dynamic_slice_in_dim(grad_out, core * half, half, 0))
    theirs = swap(mine, "core")
    sources = jnp.concatenate([relative_sources(), core[None]]).astype(jnp.int32)

    q0, qt0, s0 = turn(sgn, (flip0, near0, far0, swap(far0, "core")), table, bound, gq, 0, norm)
    sent0 = swap(s0, "core")
    got0 = exchange_zx(qt0)
    fold0 = fold(sgn_c, s0, sent0)
    cross0 = swap(fold0, "yl")

    q1, qt1, s1 = turn(sgn, (both1, far1), table, bound, gq, 1, norm, after=(fold0,))
    sent1 = swap(s1, "core")
    got1 = exchange_zx(qt1)
    fold1 = fold(sgn_c, s1, sent1)
    cross1 = swap(fold1, "yl")

    out_all = project((q0, q1), down_weight, after=(fold1,)).reshape(2, 2, -1, down_weight.shape[1])
    keep = lax.dynamic_index_in_dim(out_all, yl, 0, keepdims=False)
    give = lax.dynamic_index_in_dim(out_all, 1 - yl, 0, keepdims=False)
    summed = keep.astype(jnp.float32) + swap(give, "yl").astype(jnp.float32)
    keep = lax.dynamic_index_in_dim(summed, core, 0, keepdims=False)
    give = lax.dynamic_index_in_dim(summed, 1 - core, 0, keepdims=False).astype(jnp.bfloat16)
    output = (keep + swap(give, "core").astype(jnp.float32)).astype(jnp.bfloat16)

    acc = jnp.zeros((2 * got0.shape[1], grad_out.shape[1]), jnp.float32)
    acc = weight_grad(sources, got0, mine, theirs, 0, acc)
    acc = weight_grad(sources, got1, mine, theirs, 1, acc)
    acc = acc.reshape(2, -1, grad_out.shape[1])
    keep = lax.dynamic_index_in_dim(acc, yh, 0, keepdims=False)
    give = lax.dynamic_index_in_dim(acc, 1 - yh, 0, keepdims=False).astype(jnp.bfloat16)
    inv_root = 1.0 / math.sqrt(tok_count * n_data)
    grad_weight = (keep + swap(give, "yh").astype(jnp.float32)) * inv_root

    grad_hidden = finish(sgn_y, fold0, cross0, sign_bits, 0)
    grad_hidden = finish(sgn_y, fold1, cross1, sign_bits, 1, into=grad_hidden)
    return (output, grad_hidden, grad_weight)


def solution(mesh):
    fine = Mesh(mesh.devices.reshape(2, 8, 4, 2, 2), AXES)
    dp, tensor = ("yh", "z", "x"), ("yl", "core")
    return jax.shard_map(
        local,
        mesh=fine,
        in_specs=(P(dp, tensor), P(tensor), P(dp, tensor), P(tensor, None), P(dp, None)),
        out_specs=(P(dp + tensor, None), P(dp, tensor), P(tensor + dp, None)),
        check_vma=False,
    )
```

```python
import functools
import math

import jax
import jax.numpy as jnp
import numpy as np
from jax import lax
from jax.experimental import pallas as pl
from jax.experimental.pallas import tpu as pltpu
from jax.sharding import Mesh
from jax.sharding import PartitionSpec as P

AXES = ("yh", "z", "x", "yl", "core")
BLOCK = 896
LANES = 128
VM = pl.BlockSpec(memory_space=pltpu.VMEM)
SM = pl.BlockSpec(memory_space=pltpu.SMEM)
ANY = pl.BlockSpec(memory_space=pl.ANY)


def paley_table():
    squares_set = set((factor * factor % 13 for factor in range(1, 13)))
    core_matrix = np.zeros((14, 14))
    core_matrix[0, 1:] = 1.0
    core_matrix[1:, 0] = 1.0
    for row_idx in range(13):
        for col_idx in range(13):
            offset = (col_idx - row_idx) % 13
            if offset != 0:
                core_matrix[row_idx + 1, col_idx + 1] = 1.0 if offset in squares_set else -1.0
    first_pat = np.array([[1.0, -1.0], [-1.0, -1.0]])
    second_pat = np.array([[1.0, 1.0], [1.0, -1.0]])
    return np.kron(core_matrix, first_pat) + np.kron(np.eye(14), second_pat)


def sylvester_table(order):
    result = np.ones((1, 1))
    base_pat = np.array([[1.0, 1.0], [1.0, -1.0]])
    while result.shape[0] < order:
        result = np.kron(base_pat, result)
    return result


def block_table():
    return np.kron(sylvester_table(BLOCK // 28), paley_table())


def swap(value, axis):
    return lax.ppermute(value, axis, [(0, 1), (1, 0)])


def xor(value, axes, by):
    size = math.prod(lax.axis_size(a) for a in axes)
    return lax.ppermute(value, axes, [(i, i ^ by) for i in range(size)])


def shift(value, axis, by):
    size = lax.axis_size(axis)
    return lax.ppermute(value, axis, [(i, (i + by) % size) for i in range(size)])


def params(mib):
    return pltpu.CompilerParams(vmem_limit_bytes=mib * 2**20)


def cost(flops, nbytes):
    return pl.CostEstimate(flops=flops, bytes_accessed=nbytes, transcendentals=0)


def butterfly(parts):
    parts = list(parts)
    step = 1
    while step < len(parts):
        for base in range(len(parts)):
            if base & step == 0:
                a, b = parts[base], parts[base + step]
                parts[base], parts[base + step] = a + b, a - b
        step *= 2
    return parts


def flip_kernel(idx_ref, m_ref, p_ref, sign_ref, *rest):
    mo_ref, po_ref = rest[-2:]
    sign = (2 * sign_ref[...] - 1).astype(jnp.float32)
    mo_ref[...] = (m_ref[...].astype(jnp.float32) * sign).astype(jnp.bfloat16)
    po_ref[...] = (p_ref[...].astype(jnp.float32) * sign).astype(jnp.bfloat16)


def flip(idx, hidden, sign_bits, rows, after=()):
    cols = hidden.shape[1]
    wide = 2 * BLOCK
    block = pl.BlockSpec((rows, wide), lambda j, idx: (0, j))
    return pl.pallas_call(
        flip_kernel,
        grid_spec=pltpu.PrefetchScalarGridSpec(
            num_scalar_prefetch=1,
            grid=(cols // wide,),
            in_specs=[
                pl.BlockSpec((rows, wide), lambda j, idx: (idx[0], j)),
                pl.BlockSpec((rows, wide), lambda j, idx: (idx[1], j)),
                pl.BlockSpec((1, wide), lambda j, idx: (0, j)),
            ]
            + [ANY] * len(after),
            out_specs=(block, block),
        ),
        out_shape=(pltpu.HBM((rows, cols), jnp.bfloat16),) * 2,
        compiler_params=params(16),
        cost_estimate=cost(2 * rows * cols, 8 * rows * cols),
        name="flip",
    )(idx, hidden, hidden, sign_bits, *after)


def finish_kernel(idx_ref, sgn_ref, a_ref, b_ref, c_ref, d_ref, sign_ref, out_ref):
    rows, cols = a_ref.shape
    for at in range(0, cols, BLOCK):
        here = pl.ds(at, BLOCK)
        sign = (2 * sign_ref[:, here] - 1).astype(jnp.float32)
        for i, (own, other) in enumerate(((a_ref, b_ref), (c_ref, d_ref))):
            total = sgn_ref[0] * own[:, here].astype(jnp.float32) + other[:, here].astype(jnp.float32)
            start = pl.multiple_of(idx_ref[i] * rows, rows)
            out_ref[pl.ds(start, rows), here] = (total * sign).astype(jnp.bfloat16)


def finish(idx, sgn, mine, part, sign_bits):
    rows, cols = mine[0].shape
    return pl.pallas_call(
        finish_kernel,
        out_shape=jax.ShapeDtypeStruct((2 * rows, cols), jnp.bfloat16),
        in_specs=[SM, SM] + [VM] * 5,
        out_specs=VM,
        compiler_params=params(16),
        cost_estimate=cost(4 * rows * cols, 12 * rows * cols),
        name="finish",
    )(idx, sgn, *mine, *part, sign_bits)


def back_kernel(m_ref, p_ref, w_ref, *rest):
    mo_ref, po_ref = rest[-2:]
    rows = m_ref.shape[0]
    grads = jnp.concatenate([m_ref[...], p_ref[...]], axis=0)
    grad = lax.dot_general(grads, w_ref[...], (((1,), (1,)), ((), ())), preferred_element_type=jnp.float32)
    grad = grad.astype(jnp.bfloat16)
    mo_ref[...] = grad[:rows]
    po_ref[...] = grad[rows:]


def back(mine, part, weight, after=()):
    rows, wide = mine.shape
    cols = weight.shape[0]
    whole = pl.BlockSpec((rows, wide), lambda j: (0, 0))
    block = pl.BlockSpec((rows, BLOCK), lambda j: (0, j))
    return pl.pallas_call(
        back_kernel,
        grid=(cols // BLOCK,),
        out_shape=(pltpu.HBM((rows, cols), jnp.bfloat16),) * 2,
        in_specs=[whole, whole, pl.BlockSpec((BLOCK, wide), lambda j: (j, 0))] + [ANY] * len(after),
        out_specs=(block, block),
        compiler_params=params(24),
        cost_estimate=cost(4 * rows * cols * wide, 2 * cols * wide + 4 * rows * cols),
        name="back",
    )(mine, part, weight, *after)


def project_kernel(n, *refs):
    w_ref, out_ref, acc_ref = refs[n], refs[-2], refs[-1]
    j = pl.program_id(0)
    quant = jnp.concatenate([r[...] for r in refs[:n]], axis=0)
    part = jnp.dot(quant, w_ref[...], preferred_element_type=jnp.float32)

    @pl.when(j == 0)
    def _():
        acc_ref[...] = part

    @pl.when(j > 0)
    def _():
        acc_ref[...] += part

    @pl.when(j == pl.num_programs(0) - 1)
    def _():
        out_ref[...] = acc_ref[...].astype(out_ref.dtype)


def project(quants, weight, after=()):
    rows, cols = quants[0].shape
    n, wide = len(quants), weight.shape[1]
    block = pl.BlockSpec((rows, BLOCK), lambda j: (0, j))
    return pl.pallas_call(
        functools.partial(project_kernel, n),
        grid=(cols // BLOCK,),
        out_shape=jax.ShapeDtypeStruct((n * rows, wide), jnp.bfloat16),
        in_specs=[block] * n + [pl.BlockSpec((BLOCK, wide), lambda j: (j, 0))] + [ANY] * len(after),
        out_specs=pl.BlockSpec((n * rows, wide), lambda j: (0, 0)),
        scratch_shapes=[pltpu.VMEM((n * rows, wide), jnp.float32)],
        compiler_params=params(24),
        cost_estimate=cost(2 * n * rows * cols * wide, 2 * cols * wide),
        name="project",
    )(*quants, weight, *after)


SUB = 32


def turn_kernel(nblk, norm, sgn_ref, core_ref, own_ref, near_ref, far_ref, diag_ref, table_ref, *refs):
    bounds, (gq_here_ref, gq_there_ref) = refs[:2], refs[2:4]
    q_here_ref, q_there_ref, qt_ref, u_ref, w_ref, spun_ref = refs[-6:]
    rows = own_ref.shape[0]
    so_core, so_y = sgn_ref[0], sgn_ref[1]
    core = core_ref[0]
    span = nblk * rows
    per = BLOCK // LANES
    slabs = LANES // rows
    each = nblk // slabs
    n_dest, dest_rows = qt_ref.shape[0] // 2, qt_ref.shape[1]
    for j in range(nblk):
        cols = pl.ds(j * BLOCK, BLOCK)
        own, near, far, diag = (r[:, cols].astype(jnp.float32) for r in (own_ref, near_ref, far_ref, diag_ref))
        here = so_y * (so_core * own + near) + (so_core * far + diag)
        there = so_y * (own - so_core * near) + (far - so_core * diag)
        w_ref[pl.ds(j * rows, rows), :] = here.astype(jnp.bfloat16)
        w_ref[pl.ds(span + j * rows, rows), :] = there.astype(jnp.bfloat16)
    spun_ref[...] = jnp.dot(w_ref[...], table_ref[...], preferred_element_type=jnp.float32)

    def side(which, sub, lane, q_ref):
        toks = pl.ds(sub * SUB, SUB)
        lcols = pl.ds(lane * LANES, LANES)
        parts = butterfly([spun_ref[pl.ds(which * span + j * rows + sub * SUB, SUB), lcols] for j in range(nblk)])
        grads = []
        for j in range(nblk):
            bound = bounds[which][toks, j * per + lane : j * per + lane + 1]
            ratio = jnp.tanh(parts[j] * (norm / bound))
            cols = pl.ds(j * BLOCK + lane * LANES, LANES)
            q_ref[toks, cols] = (bound * ratio).astype(jnp.bfloat16)
            if which == 0:
                grad = gq_here_ref[toks, cols]
            else:
                grad = gq_there_ref[toks, cols]
            grads.append(grad.astype(jnp.float32) * (1.0 - ratio * ratio))
        return grads

    def transpose(lane, q_ref, slot):
        for part in range(each):
            cols = [pl.ds((slab * each + part) * BLOCK + lane * LANES, LANES) for slab in range(slabs)]
            both = jnp.concatenate([q_ref[:, c].astype(jnp.float32) for c in cols], axis=0)
            both = both.T.astype(jnp.bfloat16)
            start, done = (part * per + lane) * LANES, 0
            while done < LANES:
                dest, off = divmod(start + done, dest_rows)
                n = min(LANES - done, dest_rows - off)
                qt_ref[slot * n_dest + dest, off : off + n, :] = both[done : done + n]
                done += n

    for lane in range(per):
        lcols = pl.ds(lane * LANES, LANES)
        for sub in range(rows // SUB):
            here = side(0, sub, lane, q_here_ref)
            there = side(1, sub, lane, q_there_ref)
            for j in range(nblk):
                at = j * rows + sub * SUB
                u_ref[pl.ds(at, SUB), lcols] = (so_core * here[j] + there[j]).astype(jnp.bfloat16)
                u_ref[pl.ds(span + at, SUB), lcols] = (here[j] - so_core * there[j]).astype(jnp.bfloat16)
        transpose(lane, q_here_ref, core)
        transpose(lane, q_there_ref, 1 - core)


def turn(sgn, core, ins, table, bounds, gqs, norm, n_dest):
    rows, cols = ins[0].shape
    nblk = cols // BLOCK
    deep = 2 * nblk * rows
    flat = pltpu.HBM((rows, cols), jnp.bfloat16)
    qt = pltpu.HBM((n_dest, 2 * cols * rows // LANES // n_dest, LANES), jnp.bfloat16)
    return pl.pallas_call(
        functools.partial(turn_kernel, nblk, norm),
        out_shape=(flat, flat, qt, pltpu.HBM((deep, BLOCK), jnp.bfloat16)),
        in_specs=[SM, SM] + [VM] * 9,
        out_specs=(VM,) * 4,
        scratch_shapes=[pltpu.VMEM((deep, BLOCK), jnp.bfloat16), pltpu.VMEM((deep, BLOCK), jnp.float32)],
        compiler_params=params(32),
        cost_estimate=cost(2 * deep * BLOCK * BLOCK, 2 * rows * cols * 10),
        name="turn",
    )(sgn, core, *ins, table, *bounds, *gqs)


def return_kernel(nblk, norm, u_ref, table_ref, here_ref, there_ref, spun_ref):
    rows = here_ref.shape[0]
    span = nblk * rows
    spun_ref[...] = jnp.dot(u_ref[...], table_ref[...], preferred_element_type=jnp.float32)
    for which, v_ref in enumerate((here_ref, there_ref)):
        for sub in range(rows // SUB):
            for lane in range(BLOCK // LANES):
                lcols = pl.ds(lane * LANES, LANES)
                parts = butterfly(
                    [spun_ref[pl.ds(which * span + j * rows + sub * SUB, SUB), lcols] for j in range(nblk)]
                )
                for j in range(nblk):
                    cols = pl.ds(j * BLOCK + lane * LANES, LANES)
                    v_ref[pl.ds(sub * SUB, SUB), cols] = (parts[j] * norm).astype(jnp.bfloat16)


def turn_back(grads, table, rows, cols, norm):
    deep = grads.shape[0]
    flat = pltpu.HBM((rows, cols), jnp.bfloat16)
    return pl.pallas_call(
        functools.partial(return_kernel, cols // BLOCK, norm),
        out_shape=(flat, flat),
        in_specs=[VM, VM],
        out_specs=(VM, VM),
        scratch_shapes=[pltpu.VMEM((deep, BLOCK), jnp.float32)],
        compiler_params=params(24),
        cost_estimate=cost(2 * deep * BLOCK * BLOCK, 4 * rows * cols * 2),
        name="turn_back",
    )(grads, table)


def weight_grad_kernel(rows, toks, at_ref, r_ref, *refs):
    grad_refs, (out_ref, lhs_ref, rhs_ref) = refs[:-3], refs[-3:]
    slabs = LANES // toks
    slab = lax.broadcasted_iota(jnp.int32, (rows, LANES), 1) // toks
    blocks = [(ref, at) for ref in grad_refs for at in range(0, ref.shape[0], toks)]
    for place, (ref, start) in enumerate(blocks):
        value = r_ref[at_ref[place]]
        zero = jnp.zeros_like(value)
        at = place * LANES
        grads = ref[pl.ds(start, toks), :]
        for i in range(slabs):
            lhs_ref[i * rows : (i + 1) * rows, pl.ds(at, LANES)] = jnp.where(slab == i, value, zero)
            rhs_ref[pl.ds(at + i * toks, toks), :] = grads
    out_ref[...] = jnp.dot(lhs_ref[...], rhs_ref[...], preferred_element_type=jnp.float32)


def weight_grad(places, received, grads, toks):
    nsrc, rows, _ = received.shape
    wide = grads[0].shape[1]
    slabs = LANES // toks
    return pl.pallas_call(
        functools.partial(weight_grad_kernel, rows, toks),
        out_shape=jax.ShapeDtypeStruct((slabs * rows, wide), jnp.float32),
        in_specs=[SM] + [VM] * (1 + len(grads)),
        out_specs=VM,
        scratch_shapes=[
            pltpu.VMEM((slabs * rows, nsrc * LANES), jnp.bfloat16),
            pltpu.VMEM((nsrc * LANES, wide), jnp.bfloat16),
        ],
        compiler_params=params(40),
        cost_estimate=cost(2 * slabs * rows * nsrc * LANES * wide, 2 * nsrc * LANES * (rows + wide)),
        name="weight_grad",
    )(places, received, *grads)


def gather_z(value, *gates):
    two = after(jnp.concatenate([value, xor(value, ("z",), 4)], axis=0), *gates)
    return jnp.concatenate([two] + [xor(two, ("z",), d) for d in (1, 2, 3)], axis=0)


def gather_x(line):
    half = line.shape[0] // 2
    below, above = shift(line, "x", 1), shift(line, "x", -1)
    return [line, below, above, shift(below[:half], "x", 1), shift(above[half:], "x", -1)]


def source_places():
    nz, nx = lax.axis_size("z"), lax.axis_size("x")
    core = (lax.axis_index("core") ^ jnp.arange(2))[:, None, None]
    z = (lax.axis_index("z") ^ jnp.asarray([0, 4, 1, 5, 2, 6, 3, 7]))[None, None, :]
    x = ((lax.axis_index("x") - jnp.asarray([0, 1, -1, -2])) & (nx - 1))[None, :, None]
    return ((core * nz + z) * nx + x).reshape(-1).astype(jnp.int32)


def after(value, *others):
    return lax.optimization_barrier((value,) + others)[0]


def local(hidden, sign_bits, exponents, down_weight, grad_out):
    tok_count, ff_local = hidden.shape
    d_out = grad_out.shape[1]
    n_tensor = lax.axis_size("yl") * lax.axis_size("core")
    n_data = math.prod(lax.axis_size(a) for a in ("yh", "z", "x"))
    norm = 1.0 / math.sqrt(ff_local * n_tensor)
    half, quarter = tok_count // 2, tok_count // 4
    table = jnp.asarray(block_table(), jnp.bfloat16)
    sign_bits = sign_bits.reshape(1, ff_local)
    core, yl, yh = (lax.axis_index(a) for a in ("core", "yl", "yh"))
    so_core = (1 - 2 * core).astype(jnp.float32)
    so_y = (1 - 2 * yl).astype(jnp.float32)
    sgn_y, sgn = so_y[None], jnp.stack([so_core, so_y])
    core_at = core[None].astype(jnp.int32)
    idx = jnp.stack([core, 1 - core]).astype(jnp.int32)

    def of_mine(value):
        return lax.dynamic_slice_in_dim(value, core * half, half, 0)

    def of_part(value):
        return lax.dynamic_slice_in_dim(value, (1 - core) * half, half, 0)

    def diagonal(value):
        return xor(value, ("yl", "core"), 3)

    own, part = flip(idx, hidden, sign_bits, half)
    far, diag, near = swap(own, "yl"), diagonal(part), swap(part, "core")

    go_mine, go_part = of_mine(grad_out), of_part(grad_out)
    line = gather_z(after(go_mine, own))
    gq_here, gq_give = back(go_mine, go_part, down_weight, after=(own,))
    gq_there = swap(gq_give, "core")
    bound = 448.0 * jnp.exp2(exponents.astype(jnp.float32))
    bounds = (of_mine(bound), swap(of_part(bound), "core"))
    pieces = gather_x(after(line, far, gq_here))

    q_here, q_there, qt, grads = turn(
        sgn, core_at, (own, near, far, diag), table, bounds, (gq_here, gq_there), norm, 64
    )
    got = lax.all_to_all(after(qt, *pieces), ("core", "z", "x"), 0, 0, tiled=True)
    v_here, v_there = turn_back(grads, table, half, ff_local, norm)
    cross, dcross, ncross = swap(v_here, "yl"), diagonal(v_there), swap(v_there, "core")
    out_all = project((q_here, swap(q_there, "core")), down_weight, after=(v_here,)).reshape(2, 2, quarter, d_out)
    keep = lax.dynamic_index_in_dim(out_all, yl ^ core, 0, keepdims=False)
    give = lax.dynamic_index_in_dim(out_all, 1 - (yl ^ core), 0, keepdims=False)
    summed = keep.astype(jnp.float32) + swap(give, "yl").astype(jnp.float32)
    keep = lax.dynamic_index_in_dim(summed, core, 0, keepdims=False)
    give = lax.dynamic_index_in_dim(summed, 1 - core, 0, keepdims=False).astype(jnp.bfloat16)
    output = (keep + swap(give, "core").astype(jnp.float32)).astype(jnp.bfloat16)

    grad_hidden = finish(idx, sgn_y, (v_here, cross), (ncross, dcross), sign_bits)

    grads_all = pieces + [swap(p, "core") for p in pieces]
    acc = weight_grad(source_places(), got, grads_all, half)
    acc = acc.reshape(2, -1, d_out)
    keep = lax.dynamic_index_in_dim(acc, yh, 0, keepdims=False)
    give = lax.dynamic_index_in_dim(acc, 1 - yh, 0, keepdims=False).astype(jnp.bfloat16)
    grad_weight = (keep + swap(give, "yh").astype(jnp.float32)) * (1.0 / math.sqrt(tok_count * n_data))
    return (output, grad_hidden, grad_weight)


def solution(mesh):
    fine = Mesh(mesh.devices.reshape(2, 8, 4, 2, 2), AXES)
    dp, tensor = ("yh", "z", "x"), ("yl", "core")
    return jax.shard_map(
        local,
        mesh=fine,
        in_specs=(P(dp, tensor), P(tensor), P(dp, tensor), P(tensor, None), P(dp, None)),
        out_specs=(P(dp + tensor, None), P(dp, tensor), P(tensor + dp, None)),
        check_vma=False,
    )
```

```python
import functools
import math

import jax
import jax.numpy as jnp
import numpy as np
from jax import lax
from jax.experimental import pallas as pl
from jax.experimental.pallas import tpu as pltpu
from jax.sharding import Mesh
from jax.sharding import PartitionSpec as P

AXES = ("yh", "z", "x", "yl", "core")
BLOCK = 896
LANES = 128
VM = pl.BlockSpec(memory_space=pltpu.VMEM)
SM = pl.BlockSpec(memory_space=pltpu.SMEM)
ANY = pl.BlockSpec(memory_space=pl.ANY)


def paley_table():
    squares_set = set((factor * factor % 13 for factor in range(1, 13)))
    core_matrix = np.zeros((14, 14))
    core_matrix[0, 1:] = 1.0
    core_matrix[1:, 0] = 1.0
    for row_idx in range(13):
        for col_idx in range(13):
            offset = (col_idx - row_idx) % 13
            if offset != 0:
                core_matrix[row_idx + 1, col_idx + 1] = 1.0 if offset in squares_set else -1.0
    first_pat = np.array([[1.0, -1.0], [-1.0, -1.0]])
    second_pat = np.array([[1.0, 1.0], [1.0, -1.0]])
    return np.kron(core_matrix, first_pat) + np.kron(np.eye(14), second_pat)


def sylvester_table(order):
    result = np.ones((1, 1))
    base_pat = np.array([[1.0, 1.0], [1.0, -1.0]])
    while result.shape[0] < order:
        result = np.kron(base_pat, result)
    return result


def block_table():
    return np.kron(sylvester_table(BLOCK // 28), paley_table())


def swap(value, axis):
    return lax.ppermute(value, axis, [(0, 1), (1, 0)])


def xor(value, axes, by):
    size = math.prod(lax.axis_size(a) for a in axes)
    return lax.ppermute(value, axes, [(i, i ^ by) for i in range(size)])


def shift(value, axis, by):
    size = lax.axis_size(axis)
    return lax.ppermute(value, axis, [(i, (i + by) % size) for i in range(size)])


def params(mib):
    return pltpu.CompilerParams(vmem_limit_bytes=mib * 2**20)


def cost(flops, nbytes):
    return pl.CostEstimate(flops=flops, bytes_accessed=nbytes, transcendentals=0)


def butterfly(parts):
    parts = list(parts)
    step = 1
    while step < len(parts):
        for base in range(len(parts)):
            if base & step == 0:
                a, b = parts[base], parts[base + step]
                parts[base], parts[base + step] = a + b, a - b
        step *= 2
    return parts


def flip_kernel(idx_ref, h_ref, sign_ref, *rest):
    sign = (2 * sign_ref[...] - 1).astype(jnp.float32)
    rest[-1][...] = (h_ref[...].astype(jnp.float32) * sign).astype(jnp.bfloat16)


def flip(idx, which, hidden, sign_bits, rows, after=()):
    cols = hidden.shape[1]
    return pl.pallas_call(
        flip_kernel,
        grid_spec=pltpu.PrefetchScalarGridSpec(
            num_scalar_prefetch=1,
            grid=(1,),
            in_specs=[
                pl.BlockSpec((rows, cols), lambda i, idx: (idx[which], 0)),
                pl.BlockSpec((1, cols), lambda i, idx: (0, 0)),
            ]
            + [ANY] * len(after),
            out_specs=pl.BlockSpec((rows, cols), lambda i, idx: (0, 0)),
        ),
        out_shape=jax.ShapeDtypeStruct((rows, cols), jnp.bfloat16),
        compiler_params=params(16),
        cost_estimate=cost(rows * cols, 4 * rows * cols),
        name="flip",
    )(idx, hidden, sign_bits, *after)


def finish_kernel(idx_ref, sgn_ref, own_ref, other_ref, sign_ref, *rest):
    sign = (2 * sign_ref[...] - 1).astype(jnp.float32)
    total = sgn_ref[0] * own_ref[...].astype(jnp.float32) + other_ref[...].astype(jnp.float32)
    rest[-1][...] = (total * sign).astype(jnp.bfloat16)


def finish(idx, which, sgn, own, other, sign_bits, into=None):
    rows, cols = own.shape
    block = pl.BlockSpec((rows, cols), lambda i, idx: (0, 0))
    more = [] if into is None else [into]
    return pl.pallas_call(
        finish_kernel,
        grid_spec=pltpu.PrefetchScalarGridSpec(
            num_scalar_prefetch=1,
            grid=(1,),
            in_specs=[SM, block, block, pl.BlockSpec((1, cols), lambda i, idx: (0, 0))] + [ANY] * len(more),
            out_specs=pl.BlockSpec((rows, cols), lambda i, idx: (idx[which], 0)),
        ),
        out_shape=pltpu.HBM((2 * rows, cols), jnp.bfloat16),
        input_output_aliases={5: 0} if more else {},
        compiler_params=params(16),
        cost_estimate=cost(2 * rows * cols, 6 * rows * cols),
        name="finish",
    )(idx, sgn, own, other, sign_bits, *more)


def back_kernel(m_ref, p_ref, w_ref, *rest):
    mo_ref, po_ref = rest[-2:]
    rows = m_ref.shape[0]
    grads = jnp.concatenate([m_ref[...], p_ref[...]], axis=0)
    grad = lax.dot_general(grads, w_ref[...], (((1,), (1,)), ((), ())), preferred_element_type=jnp.float32)
    grad = grad.astype(jnp.bfloat16)
    mo_ref[...] = grad[:rows]
    po_ref[...] = grad[rows:]


def back(mine, part, weight, after=()):
    rows, wide = mine.shape
    cols = weight.shape[0]
    whole = pl.BlockSpec((rows, wide), lambda j: (0, 0))
    block = pl.BlockSpec((rows, BLOCK), lambda j: (0, j))
    return pl.pallas_call(
        back_kernel,
        grid=(cols // BLOCK,),
        out_shape=(pltpu.HBM((rows, cols), jnp.bfloat16),) * 2,
        in_specs=[whole, whole, pl.BlockSpec((BLOCK, wide), lambda j: (j, 0))] + [ANY] * len(after),
        out_specs=(block, block),
        compiler_params=params(24),
        cost_estimate=cost(4 * rows * cols * wide, 2 * cols * wide + 4 * rows * cols),
        name="back",
    )(mine, part, weight, *after)


def project_kernel(n, *refs):
    w_ref, out_ref, acc_ref = refs[n], refs[-2], refs[-1]
    j = pl.program_id(0)
    quant = jnp.concatenate([r[...] for r in refs[:n]], axis=0)
    part = jnp.dot(quant, w_ref[...], preferred_element_type=jnp.float32)

    @pl.when(j == 0)
    def _():
        acc_ref[...] = part

    @pl.when(j > 0)
    def _():
        acc_ref[...] += part

    @pl.when(j == pl.num_programs(0) - 1)
    def _():
        out_ref[...] = acc_ref[...].astype(out_ref.dtype)


def project(quants, weight, after=()):
    rows, cols = quants[0].shape
    n, wide = len(quants), weight.shape[1]
    block = pl.BlockSpec((rows, BLOCK), lambda j: (0, j))
    return pl.pallas_call(
        functools.partial(project_kernel, n),
        grid=(cols // BLOCK,),
        out_shape=jax.ShapeDtypeStruct((n * rows, wide), jnp.bfloat16),
        in_specs=[block] * n + [pl.BlockSpec((BLOCK, wide), lambda j: (j, 0))] + [ANY] * len(after),
        out_specs=pl.BlockSpec((n * rows, wide), lambda j: (0, 0)),
        scratch_shapes=[pltpu.VMEM((n * rows, wide), jnp.float32)],
        compiler_params=params(24),
        cost_estimate=cost(2 * n * rows * cols * wide, 2 * cols * wide),
        name="project",
    )(*quants, weight, *after)


SUB = 32


def turn_kernel(nblk, norm, sgn_ref, core_ref, own_ref, near_ref, far_ref, diag_ref, table_ref, *refs):
    bounds, (gq_here_ref, gq_there_ref) = refs[:2], refs[2:4]
    q_here_ref, q_there_ref, qt_ref, u_ref, w_ref, spun_ref = refs[-6:]
    rows = own_ref.shape[0]
    so_core, so_y = sgn_ref[0], sgn_ref[1]
    core = core_ref[0]
    span = nblk * rows
    per = BLOCK // LANES
    slabs = LANES // rows
    each = nblk // slabs
    n_dest, dest_rows = qt_ref.shape[0] // 2, qt_ref.shape[1]
    for j in range(nblk):
        cols = pl.ds(j * BLOCK, BLOCK)
        own, near, far, diag = (r[:, cols].astype(jnp.float32) for r in (own_ref, near_ref, far_ref, diag_ref))
        here = so_y * (so_core * own + near) + (so_core * far + diag)
        there = so_y * (own - so_core * near) + (far - so_core * diag)
        w_ref[pl.ds(j * rows, rows), :] = here.astype(jnp.bfloat16)
        w_ref[pl.ds(span + j * rows, rows), :] = there.astype(jnp.bfloat16)
    spun_ref[...] = jnp.dot(w_ref[...], table_ref[...], preferred_element_type=jnp.float32)

    def side(which, sub, lane, q_ref):
        toks = pl.ds(sub * SUB, SUB)
        lcols = pl.ds(lane * LANES, LANES)
        parts = butterfly([spun_ref[pl.ds(which * span + j * rows + sub * SUB, SUB), lcols] for j in range(nblk)])
        grads = []
        for j in range(nblk):
            bound = bounds[which][toks, j * per + lane : j * per + lane + 1]
            ratio = jnp.tanh(parts[j] * (norm / bound))
            cols = pl.ds(j * BLOCK + lane * LANES, LANES)
            q_ref[toks, cols] = (bound * ratio).astype(jnp.bfloat16)
            if which == 0:
                grad = gq_here_ref[toks, cols]
            else:
                grad = gq_there_ref[toks, cols]
            grads.append(grad.astype(jnp.float32) * (1.0 - ratio * ratio))
        return grads

    def transpose(lane, q_ref, slot):
        for part in range(each):
            cols = [pl.ds((slab * each + part) * BLOCK + lane * LANES, LANES) for slab in range(slabs)]
            both = jnp.concatenate([q_ref[:, c].astype(jnp.float32) for c in cols], axis=0)
            both = both.T.astype(jnp.bfloat16)
            start, done = (part * per + lane) * LANES, 0
            while done < LANES:
                dest, off = divmod(start + done, dest_rows)
                n = min(LANES - done, dest_rows - off)
                qt_ref[slot * n_dest + dest, off : off + n, :] = both[done : done + n]
                done += n

    for lane in range(per):
        lcols = pl.ds(lane * LANES, LANES)
        for sub in range(rows // SUB):
            here = side(0, sub, lane, q_here_ref)
            there = side(1, sub, lane, q_there_ref)
            for j in range(nblk):
                at = j * rows + sub * SUB
                u_ref[pl.ds(at, SUB), lcols] = (so_core * here[j] + there[j]).astype(jnp.bfloat16)
                u_ref[pl.ds(span + at, SUB), lcols] = (here[j] - so_core * there[j]).astype(jnp.bfloat16)
        transpose(lane, q_here_ref, core)
        transpose(lane, q_there_ref, 1 - core)


def turn(sgn, core, ins, table, bounds, gqs, norm, n_dest):
    rows, cols = ins[0].shape
    nblk = cols // BLOCK
    deep = 2 * nblk * rows
    flat = pltpu.HBM((rows, cols), jnp.bfloat16)
    qt = pltpu.HBM((n_dest, 2 * cols * rows // LANES // n_dest, LANES), jnp.bfloat16)
    return pl.pallas_call(
        functools.partial(turn_kernel, nblk, norm),
        out_shape=(flat, flat, qt, pltpu.HBM((deep, BLOCK), jnp.bfloat16)),
        in_specs=[SM, SM] + [VM] * 9,
        out_specs=(VM,) * 4,
        scratch_shapes=[pltpu.VMEM((deep, BLOCK), jnp.bfloat16), pltpu.VMEM((deep, BLOCK), jnp.float32)],
        compiler_params=params(32),
        cost_estimate=cost(2 * deep * BLOCK * BLOCK, 2 * rows * cols * 10),
        name="turn",
    )(sgn, core, *ins, table, *bounds, *gqs)


def return_kernel(nblk, norm, u_ref, table_ref, here_ref, there_ref, spun_ref):
    rows = here_ref.shape[0]
    span = nblk * rows
    spun_ref[...] = jnp.dot(u_ref[...], table_ref[...], preferred_element_type=jnp.float32)
    for which, v_ref in enumerate((here_ref, there_ref)):
        for sub in range(rows // SUB):
            for lane in range(BLOCK // LANES):
                lcols = pl.ds(lane * LANES, LANES)
                parts = butterfly(
                    [spun_ref[pl.ds(which * span + j * rows + sub * SUB, SUB), lcols] for j in range(nblk)]
                )
                for j in range(nblk):
                    cols = pl.ds(j * BLOCK + lane * LANES, LANES)
                    v_ref[pl.ds(sub * SUB, SUB), cols] = (parts[j] * norm).astype(jnp.bfloat16)


def turn_back(grads, table, rows, cols, norm):
    deep = grads.shape[0]
    flat = pltpu.HBM((rows, cols), jnp.bfloat16)
    return pl.pallas_call(
        functools.partial(return_kernel, cols // BLOCK, norm),
        out_shape=(flat, flat),
        in_specs=[VM, VM],
        out_specs=(VM, VM),
        scratch_shapes=[pltpu.VMEM((deep, BLOCK), jnp.float32)],
        compiler_params=params(24),
        cost_estimate=cost(2 * deep * BLOCK * BLOCK, 4 * rows * cols * 2),
        name="turn_back",
    )(grads, table)


def weight_grad_kernel(rows, toks, at_ref, r_ref, *refs):
    grad_refs, (out_ref, lhs_ref, rhs_ref) = refs[:-3], refs[-3:]
    slabs = LANES // toks
    slab = lax.broadcasted_iota(jnp.int32, (rows, LANES), 1) // toks
    blocks = [(ref, at) for ref in grad_refs for at in range(0, ref.shape[0], toks)]
    for place, (ref, start) in enumerate(blocks):
        value = r_ref[at_ref[place]]
        zero = jnp.zeros_like(value)
        at = place * LANES
        grads = ref[pl.ds(start, toks), :]
        for i in range(slabs):
            lhs_ref[i * rows : (i + 1) * rows, pl.ds(at, LANES)] = jnp.where(slab == i, value, zero)
            rhs_ref[pl.ds(at + i * toks, toks), :] = grads
    out_ref[...] = jnp.dot(lhs_ref[...], rhs_ref[...], preferred_element_type=jnp.float32)


def weight_grad(places, received, grads, toks):
    nsrc, rows, _ = received.shape
    wide = grads[0].shape[1]
    slabs = LANES // toks
    return pl.pallas_call(
        functools.partial(weight_grad_kernel, rows, toks),
        out_shape=jax.ShapeDtypeStruct((slabs * rows, wide), jnp.float32),
        in_specs=[SM] + [VM] * (1 + len(grads)),
        out_specs=VM,
        scratch_shapes=[
            pltpu.VMEM((slabs * rows, nsrc * LANES), jnp.bfloat16),
            pltpu.VMEM((nsrc * LANES, wide), jnp.bfloat16),
        ],
        compiler_params=params(40),
        cost_estimate=cost(2 * slabs * rows * nsrc * LANES * wide, 2 * nsrc * LANES * (rows + wide)),
        name="weight_grad",
    )(places, received, *grads)


def gather_z(value, *gates):
    two = after(jnp.concatenate([value, xor(value, ("z",), 4)], axis=0), *gates)
    return jnp.concatenate([two] + [xor(two, ("z",), d) for d in (1, 2, 3)], axis=0)


def source_places():
    nz, nx = lax.axis_size("z"), lax.axis_size("x")
    core = (lax.axis_index("core") ^ jnp.arange(2))[:, None, None]
    z = (lax.axis_index("z") ^ jnp.asarray([0, 4, 1, 5, 2, 6, 3, 7]))[None, None, :]
    x = ((lax.axis_index("x") - jnp.arange(nx)) & (nx - 1))[None, :, None]
    return ((core * nz + z) * nx + x).reshape(-1).astype(jnp.int32)


def after(value, *others):
    return lax.optimization_barrier((value,) + others)[0]


def local(hidden, sign_bits, exponents, down_weight, grad_out):
    tok_count, ff_local = hidden.shape
    d_out = grad_out.shape[1]
    n_tensor = lax.axis_size("yl") * lax.axis_size("core")
    n_data = math.prod(lax.axis_size(a) for a in ("yh", "z", "x"))
    norm = 1.0 / math.sqrt(ff_local * n_tensor)
    half, quarter = tok_count // 2, tok_count // 4
    table = jnp.asarray(block_table(), jnp.bfloat16)
    sign_bits = sign_bits.reshape(1, ff_local)
    core, yl, yh = (lax.axis_index(a) for a in ("core", "yl", "yh"))
    so_core = (1 - 2 * core).astype(jnp.float32)
    so_y = (1 - 2 * yl).astype(jnp.float32)
    sgn_y, sgn = so_y[None], jnp.stack([so_core, so_y])
    core_at = core[None].astype(jnp.int32)
    idx = jnp.stack([core, 1 - core]).astype(jnp.int32)

    def of_mine(value):
        return lax.dynamic_slice_in_dim(value, core * half, half, 0)

    def of_part(value):
        return lax.dynamic_slice_in_dim(value, (1 - core) * half, half, 0)

    def diagonal(value):
        return xor(value, ("yl", "core"), 3)

    own = flip(idx, 0, hidden, sign_bits, half)
    part = flip(idx, 1, hidden, sign_bits, half, after=(own,))
    far, diag, near = swap(own, "yl"), diagonal(part), swap(part, "core")

    go_mine, go_part = of_mine(grad_out), of_part(grad_out)
    line = gather_z(after(go_mine, own))
    gq_here, gq_give = back(go_mine, go_part, down_weight, after=(own,))
    gq_there = swap(gq_give, "core")
    bound = 448.0 * jnp.exp2(exponents.astype(jnp.float32))
    bounds = (of_mine(bound), swap(of_part(bound), "core"))
    ring = after(line, far, gq_here)
    pieces = [shift(ring, "x", s) if s else ring for s in range(4)]

    q_here, q_there, qt, grads = turn(
        sgn, core_at, (own, near, far, diag), table, bounds, (gq_here, gq_there), norm, 64
    )
    got = lax.all_to_all(after(qt, pieces[1], pieces[3]), ("core", "z", "x"), 0, 0, tiled=True)
    v_here, v_there = turn_back(grads, table, half, ff_local, norm)
    cross, ncross = swap(v_here, "yl"), swap(v_there, "core")
    early = [swap(pieces[i], "core") for i in (0, 1, 3)]

    out_all = project((q_here, swap(q_there, "core")), down_weight, after=(v_here, *early)).reshape(2, 2, quarter, d_out)
    give = lax.dynamic_index_in_dim(out_all, 1 - (yl ^ core), 0, keepdims=False)
    across = swap(give, "yl")
    dcross = diagonal(after(v_there, across))

    grad_hidden = finish(idx, 0, sgn_y, v_here, cross, sign_bits)

    late = swap(after(pieces[2], out_all), "core")
    acc = weight_grad(source_places(), after(got, grad_hidden), pieces + [early[0], early[1], late, early[2]], half)

    grad_hidden = finish(idx, 1, sgn_y, ncross, after(dcross, acc), sign_bits, into=grad_hidden)

    keep = lax.dynamic_index_in_dim(out_all, yl ^ core, 0, keepdims=False)
    summed = keep.astype(jnp.float32) + across.astype(jnp.float32)
    keep = lax.dynamic_index_in_dim(summed, core, 0, keepdims=False)
    give = lax.dynamic_index_in_dim(summed, 1 - core, 0, keepdims=False).astype(jnp.bfloat16)
    output = (keep + swap(give, "core").astype(jnp.float32)).astype(jnp.bfloat16)

    acc = acc.reshape(2, -1, d_out)
    keep = lax.dynamic_index_in_dim(acc, yh, 0, keepdims=False)
    give = lax.dynamic_index_in_dim(acc, 1 - yh, 0, keepdims=False).astype(jnp.bfloat16)
    grad_weight = (keep + swap(give, "yh").astype(jnp.float32)) * (1.0 / math.sqrt(tok_count * n_data))
    return (output, grad_hidden, grad_weight)


def solution(mesh):
    fine = Mesh(mesh.devices.reshape(2, 8, 4, 2, 2), AXES)
    dp, tensor = ("yh", "z", "x"), ("yl", "core")
    return jax.shard_map(
        local,
        mesh=fine,
        in_specs=(P(dp, tensor), P(tensor), P(dp, tensor), P(tensor, None), P(dp, None)),
        out_specs=(P(dp + tensor, None), P(dp, tensor), P(tensor + dp, None)),
        check_vma=False,
    )
```

```python
import functools
import math

import jax
import jax.numpy as jnp
import numpy as np
from jax import lax
from jax.experimental import pallas as pl
from jax.experimental.pallas import tpu as pltpu
from jax.sharding import Mesh
from jax.sharding import PartitionSpec as P

AXES = ("yh", "z", "x", "yl", "core")
BLOCK = 896
LANES = 128
VM = pl.BlockSpec(memory_space=pltpu.VMEM)
SM = pl.BlockSpec(memory_space=pltpu.SMEM)
ANY = pl.BlockSpec(memory_space=pl.ANY)


def paley_table():
    squares_set = set((factor * factor % 13 for factor in range(1, 13)))
    core_matrix = np.zeros((14, 14))
    core_matrix[0, 1:] = 1.0
    core_matrix[1:, 0] = 1.0
    for row_idx in range(13):
        for col_idx in range(13):
            offset = (col_idx - row_idx) % 13
            if offset != 0:
                core_matrix[row_idx + 1, col_idx + 1] = 1.0 if offset in squares_set else -1.0
    first_pat = np.array([[1.0, -1.0], [-1.0, -1.0]])
    second_pat = np.array([[1.0, 1.0], [1.0, -1.0]])
    return np.kron(core_matrix, first_pat) + np.kron(np.eye(14), second_pat)


def sylvester_table(order):
    result = np.ones((1, 1))
    base_pat = np.array([[1.0, 1.0], [1.0, -1.0]])
    while result.shape[0] < order:
        result = np.kron(base_pat, result)
    return result


def block_table():
    return np.kron(sylvester_table(BLOCK // 28), paley_table())


def swap(value, axis):
    return lax.ppermute(value, axis, [(0, 1), (1, 0)])


def xor(value, axes, by):
    size = math.prod(lax.axis_size(a) for a in axes)
    return lax.ppermute(value, axes, [(i, i ^ by) for i in range(size)])


def shift(value, axis, by):
    size = lax.axis_size(axis)
    return lax.ppermute(value, axis, [(i, (i + by) % size) for i in range(size)])


def in_hbm(value):
    return pltpu.with_memory_space_constraint(value, pltpu.HBM)


def params(mib):
    return pltpu.CompilerParams(vmem_limit_bytes=mib * 2**20)


def cost(flops, nbytes):
    return pl.CostEstimate(flops=flops, bytes_accessed=nbytes, transcendentals=0)


def butterfly(parts):
    parts = list(parts)
    step = 1
    while step < len(parts):
        for base in range(len(parts)):
            if base & step == 0:
                a, b = parts[base], parts[base + step]
                parts[base], parts[base + step] = a + b, a - b
        step *= 2
    return parts


def flip_kernel(idx_ref, h_ref, sign_ref, *rest):
    sign = (2 * sign_ref[...] - 1).astype(jnp.float32)
    rest[-1][...] = (h_ref[...].astype(jnp.float32) * sign).astype(jnp.bfloat16)


def flip(idx, which, hidden, sign_bits, rows, after=()):
    cols = hidden.shape[1]
    return pl.pallas_call(
        flip_kernel,
        grid_spec=pltpu.PrefetchScalarGridSpec(
            num_scalar_prefetch=1,
            grid=(1,),
            in_specs=[
                pl.BlockSpec((rows, cols), lambda i, idx: (idx[which], 0)),
                pl.BlockSpec((1, cols), lambda i, idx: (0, 0)),
            ]
            + [ANY] * len(after),
            out_specs=pl.BlockSpec((rows, cols), lambda i, idx: (0, 0)),
        ),
        out_shape=jax.ShapeDtypeStruct((rows, cols), jnp.bfloat16),
        compiler_params=params(16),
        cost_estimate=cost(rows * cols, 4 * rows * cols),
        name="flip",
    )(idx, hidden, sign_bits, *after)


def finish_kernel(idx_ref, sgn_ref, own_ref, other_ref, sign_ref, *rest):
    out_ref = rest[-1]
    for at in range(0, out_ref.shape[1], BLOCK):
        here = pl.ds(at, BLOCK)
        sign = (2 * sign_ref[:, here] - 1).astype(jnp.float32)
        total = sgn_ref[0] * own_ref[:, here].astype(jnp.float32) + other_ref[:, here].astype(jnp.float32)
        out_ref[:, here] = (total * sign).astype(jnp.bfloat16)


def finish(idx, which, sgn, own, other, sign_bits, into=None):
    rows, cols = own.shape
    block = pl.BlockSpec((rows, cols), lambda i, idx: (0, 0))
    more = [] if into is None else [into]
    return pl.pallas_call(
        finish_kernel,
        grid_spec=pltpu.PrefetchScalarGridSpec(
            num_scalar_prefetch=1,
            grid=(1,),
            in_specs=[SM, block, block, pl.BlockSpec((1, cols), lambda i, idx: (0, 0))] + [ANY] * len(more),
            out_specs=pl.BlockSpec((rows, cols), lambda i, idx: (idx[which], 0)),
        ),
        out_shape=pltpu.HBM((2 * rows, cols), jnp.bfloat16),
        input_output_aliases={5: 0} if more else {},
        compiler_params=params(16),
        cost_estimate=cost(2 * rows * cols, 6 * rows * cols),
        name="finish",
    )(idx, sgn, own, other, sign_bits, *more)


def back_kernel(m_ref, p_ref, w_ref, *rest):
    mo_ref, po_ref = rest[-2:]
    rows = m_ref.shape[0]
    grads = jnp.concatenate([m_ref[...], p_ref[...]], axis=0)
    grad = lax.dot_general(grads, w_ref[...], (((1,), (1,)), ((), ())), preferred_element_type=jnp.float32)
    grad = grad.astype(jnp.bfloat16)
    mo_ref[...] = grad[:rows]
    po_ref[...] = grad[rows:]


def back(mine, part, weight, after=()):
    rows, wide = mine.shape
    cols = weight.shape[0]
    whole = pl.BlockSpec((rows, wide), lambda j: (0, 0))
    block = pl.BlockSpec((rows, BLOCK), lambda j: (0, j))
    return pl.pallas_call(
        back_kernel,
        grid=(cols // BLOCK,),
        out_shape=(pltpu.HBM((rows, cols), jnp.bfloat16),) * 2,
        in_specs=[whole, whole, pl.BlockSpec((BLOCK, wide), lambda j: (j, 0))] + [ANY] * len(after),
        out_specs=(block, block),
        compiler_params=params(24),
        cost_estimate=cost(4 * rows * cols * wide, 2 * cols * wide + 4 * rows * cols),
        name="back",
    )(mine, part, weight, *after)


def project_kernel(n, *refs):
    w_ref, out_ref, acc_ref = refs[n], refs[-2], refs[-1]
    j = pl.program_id(0)
    quant = jnp.concatenate([r[...] for r in refs[:n]], axis=0)
    part = jnp.dot(quant, w_ref[...], preferred_element_type=jnp.float32)

    @pl.when(j == 0)
    def _():
        acc_ref[...] = part

    @pl.when(j > 0)
    def _():
        acc_ref[...] += part

    @pl.when(j == pl.num_programs(0) - 1)
    def _():
        out_ref[...] = acc_ref[...].astype(out_ref.dtype)


def project(quants, weight, after=()):
    rows, cols = quants[0].shape
    n, wide = len(quants), weight.shape[1]
    block = pl.BlockSpec((rows, BLOCK), lambda j: (0, j))
    return pl.pallas_call(
        functools.partial(project_kernel, n),
        grid=(cols // BLOCK,),
        out_shape=jax.ShapeDtypeStruct((n * rows, wide), jnp.bfloat16),
        in_specs=[block] * n + [pl.BlockSpec((BLOCK, wide), lambda j: (j, 0))] + [ANY] * len(after),
        out_specs=pl.BlockSpec((n * rows, wide), lambda j: (0, 0)),
        scratch_shapes=[pltpu.VMEM((n * rows, wide), jnp.float32)],
        compiler_params=params(24),
        cost_estimate=cost(2 * n * rows * cols * wide, 2 * cols * wide),
        name="project",
    )(*quants, weight, *after)


SUB = 32


def turn_kernel(nblk, norm, sgn_ref, core_ref, own_ref, near_ref, far_ref, diag_ref, table_ref, *refs):
    bounds, (gq_here_ref, gq_there_ref) = refs[:2], refs[2:4]
    q_here_ref, q_there_ref, qt_ref, u_ref, w_ref, spun_ref = refs[-6:]
    rows = own_ref.shape[0]
    so_core, so_y = sgn_ref[0], sgn_ref[1]
    core = core_ref[0]
    span = nblk * rows
    per = BLOCK // LANES
    slabs = LANES // rows
    each = nblk // slabs
    n_dest, dest_rows = qt_ref.shape[0] // 2, qt_ref.shape[1]
    for j in range(nblk):
        cols = pl.ds(j * BLOCK, BLOCK)
        own, near, far, diag = (r[:, cols].astype(jnp.float32) for r in (own_ref, near_ref, far_ref, diag_ref))
        here = so_y * (so_core * own + near) + (so_core * far + diag)
        there = so_y * (own - so_core * near) + (far - so_core * diag)
        w_ref[pl.ds(j * rows, rows), :] = here.astype(jnp.bfloat16)
        w_ref[pl.ds(span + j * rows, rows), :] = there.astype(jnp.bfloat16)
    spun_ref[...] = jnp.dot(w_ref[...], table_ref[...], preferred_element_type=jnp.float32)

    def side(which, sub, lane, q_ref):
        toks = pl.ds(sub * SUB, SUB)
        lcols = pl.ds(lane * LANES, LANES)
        parts = butterfly([spun_ref[pl.ds(which * span + j * rows + sub * SUB, SUB), lcols] for j in range(nblk)])
        grads = []
        for j in range(nblk):
            bound = bounds[which][toks, j * per + lane : j * per + lane + 1]
            ratio = jnp.tanh(parts[j] * (norm / bound))
            cols = pl.ds(j * BLOCK + lane * LANES, LANES)
            q_ref[toks, cols] = (bound * ratio).astype(jnp.bfloat16)
            if which == 0:
                grad = gq_here_ref[toks, cols]
            else:
                grad = gq_there_ref[toks, cols]
            grads.append(grad.astype(jnp.float32) * (1.0 - ratio * ratio))
        return grads

    def transpose(lane, q_ref, slot):
        for part in range(each):
            cols = [pl.ds((slab * each + part) * BLOCK + lane * LANES, LANES) for slab in range(slabs)]
            both = jnp.concatenate([q_ref[:, c].astype(jnp.float32) for c in cols], axis=0)
            both = both.T.astype(jnp.bfloat16)
            start, done = (part * per + lane) * LANES, 0
            while done < LANES:
                dest, off = divmod(start + done, dest_rows)
                n = min(LANES - done, dest_rows - off)
                qt_ref[slot * n_dest + dest, off : off + n, :] = both[done : done + n]
                done += n

    for lane in range(per):
        lcols = pl.ds(lane * LANES, LANES)
        for sub in range(rows // SUB):
            here = side(0, sub, lane, q_here_ref)
            there = side(1, sub, lane, q_there_ref)
            for j in range(nblk):
                at = j * rows + sub * SUB
                u_ref[pl.ds(at, SUB), lcols] = (so_core * here[j] + there[j]).astype(jnp.bfloat16)
                u_ref[pl.ds(span + at, SUB), lcols] = (here[j] - so_core * there[j]).astype(jnp.bfloat16)
        transpose(lane, q_here_ref, core)
        transpose(lane, q_there_ref, 1 - core)


def turn(sgn, core, ins, table, bounds, gqs, norm, n_dest):
    rows, cols = ins[0].shape
    nblk = cols // BLOCK
    deep = 2 * nblk * rows
    flat = pltpu.HBM((rows, cols), jnp.bfloat16)
    qt = pltpu.HBM((n_dest, 2 * cols * rows // LANES // n_dest, LANES), jnp.bfloat16)
    return pl.pallas_call(
        functools.partial(turn_kernel, nblk, norm),
        out_shape=(flat, flat, qt, pltpu.HBM((deep, BLOCK), jnp.bfloat16)),
        in_specs=[SM, SM] + [VM] * 9,
        out_specs=(VM,) * 4,
        scratch_shapes=[pltpu.VMEM((deep, BLOCK), jnp.bfloat16), pltpu.VMEM((deep, BLOCK), jnp.float32)],
        compiler_params=params(32),
        cost_estimate=cost(2 * deep * BLOCK * BLOCK, 2 * rows * cols * 10),
        name="turn",
    )(sgn, core, *ins, table, *bounds, *[in_hbm(g) for g in gqs])


def return_kernel(nblk, norm, u_ref, table_ref, here_ref, there_ref, spun_ref):
    rows = here_ref.shape[0]
    span = nblk * rows
    spun_ref[...] = jnp.dot(u_ref[...], table_ref[...], preferred_element_type=jnp.float32)
    for which, v_ref in enumerate((here_ref, there_ref)):
        for sub in range(rows // SUB):
            for lane in range(BLOCK // LANES):
                lcols = pl.ds(lane * LANES, LANES)
                parts = butterfly(
                    [spun_ref[pl.ds(which * span + j * rows + sub * SUB, SUB), lcols] for j in range(nblk)]
                )
                for j in range(nblk):
                    cols = pl.ds(j * BLOCK + lane * LANES, LANES)
                    v_ref[pl.ds(sub * SUB, SUB), cols] = (parts[j] * norm).astype(jnp.bfloat16)


def turn_back(grads, table, rows, cols, norm):
    deep = grads.shape[0]
    flat = pltpu.HBM((rows, cols), jnp.bfloat16)
    return pl.pallas_call(
        functools.partial(return_kernel, cols // BLOCK, norm),
        out_shape=(flat, flat),
        in_specs=[VM, VM],
        out_specs=(VM, VM),
        scratch_shapes=[pltpu.VMEM((deep, BLOCK), jnp.float32)],
        compiler_params=params(24),
        cost_estimate=cost(2 * deep * BLOCK * BLOCK, 4 * rows * cols * 2),
        name="turn_back",
    )(in_hbm(grads), in_hbm(table))


def weight_grad_kernel(rows, toks, at_ref, r_ref, *refs):
    grad_refs, (out_ref, lhs_ref) = refs[:-2], refs[-2:]
    low = lax.broadcasted_iota(jnp.int32, (rows, LANES), 1) < toks
    for place in range(0, r_ref.shape[0], 2):
        first, second = r_ref[at_ref[place]], r_ref[at_ref[place + 1]]
        cols = pl.ds(place * toks, LANES)
        lhs_ref[0:rows, cols] = jnp.where(low, first, jnp.roll(second, toks, 1))
        lhs_ref[rows : 2 * rows, cols] = jnp.where(low, jnp.roll(first, toks, 1), second)
    total, at = None, 0
    for ref in grad_refs:
        deep = ref.shape[0]
        part = jnp.dot(lhs_ref[:, at : at + deep], ref[...], preferred_element_type=jnp.float32)
        total, at = part if total is None else total + part, at + deep
    out_ref[...] = total


def weight_grad(places, received, grads, toks):
    nsrc, rows, _ = received.shape
    wide = grads[0].shape[1]
    return pl.pallas_call(
        functools.partial(weight_grad_kernel, rows, toks),
        out_shape=jax.ShapeDtypeStruct((2 * rows, wide), jnp.float32),
        in_specs=[SM] + [VM] * (1 + len(grads)),
        out_specs=VM,
        scratch_shapes=[pltpu.VMEM((2 * rows, nsrc * toks), jnp.bfloat16)],
        compiler_params=params(32),
        cost_estimate=cost(4 * rows * nsrc * toks * wide, 2 * nsrc * toks * (2 * rows + wide)),
        name="weight_grad",
    )(places, received, *[in_hbm(g) if g.shape[0] > 4 * toks else g for g in grads])


def gather_z(value, *gates):
    two = after(jnp.concatenate([value, xor(value, ("z",), 4)], axis=0), *gates)
    return jnp.concatenate([two] + [xor(two, ("z",), d) for d in (1, 2, 3)], axis=0)


def source_places():
    nz, nx = lax.axis_size("z"), lax.axis_size("x")
    core = (lax.axis_index("core") ^ jnp.arange(2))[:, None, None]
    z = (lax.axis_index("z") ^ jnp.asarray([0, 4, 1, 5, 2, 6, 3, 7]))[None, None, :]
    x = ((lax.axis_index("x") - jnp.arange(nx)) & (nx - 1))[None, :, None]
    return ((core * nz + z) * nx + x).reshape(-1).astype(jnp.int32)


def after(value, *others):
    return lax.optimization_barrier((value,) + others)[0]


def local(hidden, sign_bits, exponents, down_weight, grad_out):
    tok_count, ff_local = hidden.shape
    d_out = grad_out.shape[1]
    n_tensor = lax.axis_size("yl") * lax.axis_size("core")
    n_data = math.prod(lax.axis_size(a) for a in ("yh", "z", "x"))
    norm = 1.0 / math.sqrt(ff_local * n_tensor)
    half, quarter = tok_count // 2, tok_count // 4
    table = jnp.asarray(block_table(), jnp.bfloat16)
    sign_bits = sign_bits.reshape(1, ff_local)
    core, yl, yh = (lax.axis_index(a) for a in ("core", "yl", "yh"))
    so_core = (1 - 2 * core).astype(jnp.float32)
    so_y = (1 - 2 * yl).astype(jnp.float32)
    sgn_y, sgn = so_y[None], jnp.stack([so_core, so_y])
    core_at = core[None].astype(jnp.int32)
    idx = jnp.stack([core, 1 - core]).astype(jnp.int32)

    def of_mine(value):
        return lax.dynamic_slice_in_dim(value, core * half, half, 0)

    def of_part(value):
        return lax.dynamic_slice_in_dim(value, (1 - core) * half, half, 0)

    def diagonal(value):
        return xor(value, ("yl", "core"), 3)

    own = flip(idx, 0, hidden, sign_bits, half)
    part = flip(idx, 1, hidden, sign_bits, half, after=(own,))
    far, diag, near = swap(own, "yl"), diagonal(part), swap(part, "core")

    go_mine, go_part = of_mine(grad_out), of_part(grad_out)
    line = gather_z(after(go_mine, own))
    gq_here, gq_give = back(go_mine, go_part, down_weight, after=(own,))
    gq_there = swap(gq_give, "core")
    bound = 448.0 * jnp.exp2(exponents.astype(jnp.float32))
    bounds = (of_mine(bound), swap(of_part(bound), "core"))
    ring = after(line, far, gq_here)
    pieces = [ring, shift(ring, "x", 1), None, shift(ring, "x", 3)]

    q_here, q_there, qt, grads = turn(
        sgn, core_at, (own, near, far, diag), table, bounds, (gq_here, gq_there), norm, 64
    )
    got = lax.all_to_all(after(qt, pieces[1], pieces[3]), ("core", "z", "x"), 0, 0, tiled=True)
    v_here, v_there = turn_back(grads, table, half, ff_local, norm)
    pieces[2] = shift(after(ring, v_here), "x", 2)
    cross, ncross = swap(v_here, "yl"), swap(v_there, "core")
    early = [swap(pieces[i], "core") for i in (0, 1, 3)]

    out_all = project((q_here, swap(q_there, "core")), down_weight, after=(v_here, *early)).reshape(2, 2, quarter, d_out)
    give = lax.dynamic_index_in_dim(out_all, 1 - (yl ^ core), 0, keepdims=False)
    across = swap(give, "yl")
    dcross = diagonal(after(v_there, across))

    grad_hidden = finish(idx, 0, sgn_y, v_here, cross, sign_bits)

    gated = after(pieces[2], across)
    quads = gated.shape[0] // 4
    late = [swap(gated[i * quads : (i + 1) * quads], "core") for i in range(4)]
    acc = weight_grad(source_places(), after(got, grad_hidden), pieces + [early[0], early[1], *late, early[2]], half)

    grad_hidden = finish(idx, 1, sgn_y, ncross, after(dcross, acc), sign_bits, into=grad_hidden)

    keep = lax.dynamic_index_in_dim(out_all, yl ^ core, 0, keepdims=False)
    summed = keep.astype(jnp.float32) + across.astype(jnp.float32)
    keep = lax.dynamic_index_in_dim(summed, core, 0, keepdims=False)
    give = lax.dynamic_index_in_dim(summed, 1 - core, 0, keepdims=False).astype(jnp.bfloat16)
    output = (keep + swap(give, "core").astype(jnp.float32)).astype(jnp.bfloat16)

    acc = acc.reshape(2, -1, d_out)
    keep = lax.dynamic_index_in_dim(acc, yh, 0, keepdims=False)
    give = lax.dynamic_index_in_dim(acc, 1 - yh, 0, keepdims=False).astype(jnp.bfloat16)
    grad_weight = (keep + swap(give, "yh").astype(jnp.float32)) * (1.0 / math.sqrt(tok_count * n_data))
    return (output, grad_hidden, grad_weight)


def solution(mesh):
    fine = Mesh(mesh.devices.reshape(2, 8, 4, 2, 2), AXES)
    dp, tensor = ("yh", "z", "x"), ("yl", "core")
    return jax.shard_map(
        local,
        mesh=fine,
        in_specs=(P(dp, tensor), P(tensor), P(dp, tensor), P(tensor, None), P(dp, None)),
        out_specs=(P(dp + tensor, None), P(dp, tensor), P(tensor + dp, None)),
        check_vma=False,
    )
```

```python
import functools
import math

import jax
import jax.numpy as jnp
import numpy as np
from jax import lax
from jax.experimental import pallas as pl
from jax.experimental.pallas import tpu as pltpu
from jax.sharding import Mesh
from jax.sharding import PartitionSpec as P

AXES = ("yh", "z", "x", "yl", "core")
BLOCK = 896
LANES = 128
VM = pl.BlockSpec(memory_space=pltpu.VMEM)
SM = pl.BlockSpec(memory_space=pltpu.SMEM)
ANY = pl.BlockSpec(memory_space=pl.ANY)


def paley_table():
    squares_set = set((factor * factor % 13 for factor in range(1, 13)))
    core_matrix = np.zeros((14, 14))
    core_matrix[0, 1:] = 1.0
    core_matrix[1:, 0] = 1.0
    for row_idx in range(13):
        for col_idx in range(13):
            offset = (col_idx - row_idx) % 13
            if offset != 0:
                core_matrix[row_idx + 1, col_idx + 1] = 1.0 if offset in squares_set else -1.0
    first_pat = np.array([[1.0, -1.0], [-1.0, -1.0]])
    second_pat = np.array([[1.0, 1.0], [1.0, -1.0]])
    return np.kron(core_matrix, first_pat) + np.kron(np.eye(14), second_pat)


def sylvester_table(order):
    result = np.ones((1, 1))
    base_pat = np.array([[1.0, 1.0], [1.0, -1.0]])
    while result.shape[0] < order:
        result = np.kron(base_pat, result)
    return result


def block_table():
    return np.kron(sylvester_table(BLOCK // 28), paley_table())


def swap(value, axis):
    return lax.ppermute(value, axis, [(0, 1), (1, 0)])


def xor(value, axes, by):
    size = math.prod(lax.axis_size(a) for a in axes)
    return lax.ppermute(value, axes, [(i, i ^ by) for i in range(size)])


def shift(value, axis, by):
    size = lax.axis_size(axis)
    return lax.ppermute(value, axis, [(i, (i + by) % size) for i in range(size)])


def in_hbm(value):
    return pltpu.with_memory_space_constraint(value, pltpu.HBM)


def params(mib):
    return pltpu.CompilerParams(vmem_limit_bytes=mib * 2**20)


def cost(flops, nbytes):
    return pl.CostEstimate(flops=flops, bytes_accessed=nbytes, transcendentals=0)


def butterfly(parts):
    parts = list(parts)
    step = 1
    while step < len(parts):
        for base in range(len(parts)):
            if base & step == 0:
                a, b = parts[base], parts[base + step]
                parts[base], parts[base + step] = a + b, a - b
        step *= 2
    return parts


def flip_kernel(idx_ref, h_ref, sign_ref, *rest):
    sign = (2 * sign_ref[...] - 1).astype(jnp.float32)
    rest[-1][...] = (h_ref[...].astype(jnp.float32) * sign).astype(jnp.bfloat16)


def flip(idx, which, hidden, sign_bits, rows, after=()):
    cols = hidden.shape[1]
    return pl.pallas_call(
        flip_kernel,
        grid_spec=pltpu.PrefetchScalarGridSpec(
            num_scalar_prefetch=1,
            grid=(1,),
            in_specs=[
                pl.BlockSpec((rows, cols), lambda i, idx: (idx[which], 0)),
                pl.BlockSpec((1, cols), lambda i, idx: (0, 0)),
            ]
            + [ANY] * len(after),
            out_specs=pl.BlockSpec((rows, cols), lambda i, idx: (0, 0)),
        ),
        out_shape=jax.ShapeDtypeStruct((rows, cols), jnp.bfloat16),
        compiler_params=params(16),
        cost_estimate=cost(rows * cols, 4 * rows * cols),
        name="flip",
    )(idx, hidden, sign_bits, *after)


def finish_kernel(idx_ref, sgn_ref, own_ref, other_ref, sign_ref, *rest):
    out_ref = rest[-1]
    for at in range(0, out_ref.shape[1], BLOCK):
        here = pl.ds(at, BLOCK)
        sign = (2 * sign_ref[:, here] - 1).astype(jnp.float32)
        total = sgn_ref[0] * own_ref[:, here].astype(jnp.float32) + other_ref[:, here].astype(jnp.float32)
        out_ref[:, here] = (total * sign).astype(jnp.bfloat16)


def finish(idx, which, sgn, own, other, sign_bits, into=None):
    rows, cols = own.shape
    block = pl.BlockSpec((rows, cols), lambda i, idx: (0, 0))
    more = [] if into is None else [into]
    return pl.pallas_call(
        finish_kernel,
        grid_spec=pltpu.PrefetchScalarGridSpec(
            num_scalar_prefetch=1,
            grid=(1,),
            in_specs=[SM, block, block, pl.BlockSpec((1, cols), lambda i, idx: (0, 0))] + [ANY] * len(more),
            out_specs=pl.BlockSpec((rows, cols), lambda i, idx: (idx[which], 0)),
        ),
        out_shape=pltpu.HBM((2 * rows, cols), jnp.bfloat16),
        input_output_aliases={5: 0} if more else {},
        compiler_params=params(16),
        cost_estimate=cost(2 * rows * cols, 6 * rows * cols),
        name="finish",
    )(idx, sgn, own, other, sign_bits, *more)


def back_kernel(m_ref, p_ref, w_ref, *rest):
    mo_ref, po_ref = rest[-2:]
    rows = m_ref.shape[0]
    grads = jnp.concatenate([m_ref[...], p_ref[...]], axis=0)
    grad = lax.dot_general(grads, w_ref[...], (((1,), (1,)), ((), ())), preferred_element_type=jnp.float32)
    grad = grad.astype(jnp.bfloat16)
    mo_ref[...] = grad[:rows]
    po_ref[...] = grad[rows:]


def back(mine, part, weight, after=()):
    rows, wide = mine.shape
    cols = weight.shape[0]
    whole = pl.BlockSpec((rows, wide), lambda j: (0, 0))
    block = pl.BlockSpec((rows, BLOCK), lambda j: (0, j))
    return pl.pallas_call(
        back_kernel,
        grid=(cols // BLOCK,),
        out_shape=(pltpu.HBM((rows, cols), jnp.bfloat16),) * 2,
        in_specs=[whole, whole, pl.BlockSpec((BLOCK, wide), lambda j: (j, 0))] + [ANY] * len(after),
        out_specs=(block, block),
        compiler_params=params(24),
        cost_estimate=cost(4 * rows * cols * wide, 2 * cols * wide + 4 * rows * cols),
        name="back",
    )(mine, part, weight, *after)


def project_kernel(n, *refs):
    w_ref, out_ref, acc_ref = refs[n], refs[-2], refs[-1]
    j = pl.program_id(0)
    quant = jnp.concatenate([r[...] for r in refs[:n]], axis=0)
    part = jnp.dot(quant, w_ref[...], preferred_element_type=jnp.float32)

    @pl.when(j == 0)
    def _():
        acc_ref[...] = part

    @pl.when(j > 0)
    def _():
        acc_ref[...] += part

    @pl.when(j == pl.num_programs(0) - 1)
    def _():
        out_ref[...] = acc_ref[...].astype(out_ref.dtype)


def project(quants, weight, after=()):
    rows, cols = quants[0].shape
    n, wide = len(quants), weight.shape[1]
    block = pl.BlockSpec((rows, BLOCK), lambda j: (0, j))
    return pl.pallas_call(
        functools.partial(project_kernel, n),
        grid=(cols // BLOCK,),
        out_shape=jax.ShapeDtypeStruct((n * rows, wide), jnp.bfloat16),
        in_specs=[block] * n + [pl.BlockSpec((BLOCK, wide), lambda j: (j, 0))] + [ANY] * len(after),
        out_specs=pl.BlockSpec((n * rows, wide), lambda j: (0, 0)),
        scratch_shapes=[pltpu.VMEM((n * rows, wide), jnp.float32)],
        compiler_params=params(24),
        cost_estimate=cost(2 * n * rows * cols * wide, 2 * cols * wide),
        name="project",
    )(*quants, weight, *after)


SUB = 32


def turn_kernel(nblk, norm, sgn_ref, core_ref, own_ref, near_ref, far_ref, diag_ref, table_ref, *refs):
    bounds, (gq_here_ref, gq_there_ref) = refs[:2], refs[2:4]
    q_here_ref, q_there_ref, qt_ref, u_ref, w_ref, spun_ref = refs[-6:]
    rows = own_ref.shape[0]
    so_core, so_y = sgn_ref[0], sgn_ref[1]
    core = core_ref[0]
    span = nblk * rows
    per = BLOCK // LANES
    slabs = LANES // rows
    each = nblk // slabs
    n_dest, dest_rows = qt_ref.shape[0] // 2, qt_ref.shape[1]
    for j in range(nblk):
        cols = pl.ds(j * BLOCK, BLOCK)
        own, near, far, diag = (r[:, cols].astype(jnp.float32) for r in (own_ref, near_ref, far_ref, diag_ref))
        here = so_y * (so_core * own + near) + (so_core * far + diag)
        there = so_y * (own - so_core * near) + (far - so_core * diag)
        w_ref[pl.ds(j * rows, rows), :] = here.astype(jnp.bfloat16)
        w_ref[pl.ds(span + j * rows, rows), :] = there.astype(jnp.bfloat16)
    spun_ref[...] = jnp.dot(w_ref[...], table_ref[...], preferred_element_type=jnp.float32)

    def side(which, sub, lane, q_ref):
        toks = pl.ds(sub * SUB, SUB)
        lcols = pl.ds(lane * LANES, LANES)
        parts = butterfly([spun_ref[pl.ds(which * span + j * rows + sub * SUB, SUB), lcols] for j in range(nblk)])
        grads = []
        for j in range(nblk):
            bound = bounds[which][toks, j * per + lane : j * per + lane + 1]
            ratio = jnp.tanh(parts[j] * (norm / bound))
            cols = pl.ds(j * BLOCK + lane * LANES, LANES)
            q_ref[toks, cols] = (bound * ratio).astype(jnp.bfloat16)
            if which == 0:
                grad = gq_here_ref[toks, cols]
            else:
                grad = gq_there_ref[toks, cols]
            grads.append(grad.astype(jnp.float32) * (1.0 - ratio * ratio))
        return grads

    def transpose(lane, q_ref, slot):
        for part in range(each):
            cols = [pl.ds((slab * each + part) * BLOCK + lane * LANES, LANES) for slab in range(slabs)]
            both = jnp.concatenate([q_ref[:, c].astype(jnp.float32) for c in cols], axis=0)
            both = both.T.astype(jnp.bfloat16)
            start, done = (part * per + lane) * LANES, 0
            while done < LANES:
                dest, off = divmod(start + done, dest_rows)
                n = min(LANES - done, dest_rows - off)
                qt_ref[slot * n_dest + dest, off : off + n, :] = both[done : done + n]
                done += n

    for lane in range(per):
        lcols = pl.ds(lane * LANES, LANES)
        for sub in range(rows // SUB):
            here = side(0, sub, lane, q_here_ref)
            there = side(1, sub, lane, q_there_ref)
            for j in range(nblk):
                at = j * rows + sub * SUB
                u_ref[pl.ds(at, SUB), lcols] = (so_core * here[j] + there[j]).astype(jnp.bfloat16)
                u_ref[pl.ds(span + at, SUB), lcols] = (here[j] - so_core * there[j]).astype(jnp.bfloat16)
        transpose(lane, q_here_ref, core)
        transpose(lane, q_there_ref, 1 - core)


def turn(sgn, core, ins, table, bounds, gqs, norm, n_dest):
    rows, cols = ins[0].shape
    nblk = cols // BLOCK
    deep = 2 * nblk * rows
    flat = pltpu.HBM((rows, cols), jnp.bfloat16)
    qt = pltpu.HBM((n_dest, 2 * cols * rows // LANES // n_dest, LANES), jnp.bfloat16)
    return pl.pallas_call(
        functools.partial(turn_kernel, nblk, norm),
        out_shape=(flat, flat, qt, pltpu.HBM((deep, BLOCK), jnp.bfloat16)),
        in_specs=[SM, SM] + [VM] * 9,
        out_specs=(VM,) * 4,
        scratch_shapes=[pltpu.VMEM((deep, BLOCK), jnp.bfloat16), pltpu.VMEM((deep, BLOCK), jnp.float32)],
        compiler_params=params(32),
        cost_estimate=cost(2 * deep * BLOCK * BLOCK, 2 * rows * cols * 10),
        name="turn",
    )(sgn, core, *ins, table, *bounds, *[in_hbm(g) for g in gqs])


def return_kernel(nblk, norm, u_ref, table_ref, here_ref, there_ref, spun_ref):
    rows = here_ref.shape[0]
    span = nblk * rows
    spun_ref[...] = jnp.dot(u_ref[...], table_ref[...], preferred_element_type=jnp.float32)
    for which, v_ref in enumerate((here_ref, there_ref)):
        for sub in range(rows // SUB):
            for lane in range(BLOCK // LANES):
                lcols = pl.ds(lane * LANES, LANES)
                parts = butterfly(
                    [spun_ref[pl.ds(which * span + j * rows + sub * SUB, SUB), lcols] for j in range(nblk)]
                )
                for j in range(nblk):
                    cols = pl.ds(j * BLOCK + lane * LANES, LANES)
                    v_ref[pl.ds(sub * SUB, SUB), cols] = (parts[j] * norm).astype(jnp.bfloat16)


def turn_back(grads, table, rows, cols, norm):
    deep = grads.shape[0]
    flat = pltpu.HBM((rows, cols), jnp.bfloat16)
    return pl.pallas_call(
        functools.partial(return_kernel, cols // BLOCK, norm),
        out_shape=(flat, flat),
        in_specs=[VM, VM],
        out_specs=(VM, VM),
        scratch_shapes=[pltpu.VMEM((deep, BLOCK), jnp.float32)],
        compiler_params=params(24),
        cost_estimate=cost(2 * deep * BLOCK * BLOCK, 4 * rows * cols * 2),
        name="turn_back",
    )(in_hbm(grads), in_hbm(table))


def weight_grad_kernel(rows, toks, at_ref, r_ref, *refs):
    grad_refs, (out_ref, lhs_ref) = refs[:-2], refs[-2:]
    low = lax.broadcasted_iota(jnp.int32, (rows, LANES), 1) < toks
    for place in range(0, r_ref.shape[0], 2):
        first, second = r_ref[at_ref[place]], r_ref[at_ref[place + 1]]
        cols = pl.ds(place * toks, LANES)
        lhs_ref[0:rows, cols] = jnp.where(low, first, jnp.roll(second, toks, 1))
        lhs_ref[rows : 2 * rows, cols] = jnp.where(low, jnp.roll(first, toks, 1), second)
    total, at = None, 0
    for ref in grad_refs:
        deep = ref.shape[0]
        part = jnp.dot(lhs_ref[:, at : at + deep], ref[...], preferred_element_type=jnp.float32)
        total, at = part if total is None else total + part, at + deep
    out_ref[...] = total


def weight_grad(places, received, grads, toks):
    nsrc, rows, _ = received.shape
    wide = grads[0].shape[1]
    return pl.pallas_call(
        functools.partial(weight_grad_kernel, rows, toks),
        out_shape=jax.ShapeDtypeStruct((2 * rows, wide), jnp.float32),
        in_specs=[SM] + [VM] * (1 + len(grads)),
        out_specs=VM,
        scratch_shapes=[pltpu.VMEM((2 * rows, nsrc * toks), jnp.bfloat16)],
        compiler_params=params(32),
        cost_estimate=cost(4 * rows * nsrc * toks * wide, 2 * nsrc * toks * (2 * rows + wide)),
        name="weight_grad",
    )(places, received, *[in_hbm(g) if g.shape[0] > 4 * toks else g for g in grads])


def gather_z(value, *gates):
    two = after(jnp.concatenate([value, xor(value, ("z",), 4)], axis=0), *gates)
    return jnp.concatenate([two] + [xor(two, ("z",), d) for d in (1, 2, 3)], axis=0)


def source_places():
    nz, nx = lax.axis_size("z"), lax.axis_size("x")
    core = (lax.axis_index("core") ^ jnp.arange(2))[:, None, None]
    z = (lax.axis_index("z") ^ jnp.asarray([0, 4, 1, 5, 2, 6, 3, 7]))[None, None, :]
    x = ((lax.axis_index("x") - jnp.arange(nx)) & (nx - 1))[None, :, None]
    return ((core * nz + z) * nx + x).reshape(-1).astype(jnp.int32)


def after(value, *others):
    return lax.optimization_barrier((value,) + others)[0]


def local(hidden, sign_bits, exponents, down_weight, grad_out):
    tok_count, ff_local = hidden.shape
    d_out = grad_out.shape[1]
    n_tensor = lax.axis_size("yl") * lax.axis_size("core")
    n_data = math.prod(lax.axis_size(a) for a in ("yh", "z", "x"))
    norm = 1.0 / math.sqrt(ff_local * n_tensor)
    half, quarter = tok_count // 2, tok_count // 4
    table = jnp.asarray(block_table(), jnp.bfloat16)
    sign_bits = sign_bits.reshape(1, ff_local)
    core, yl, yh = (lax.axis_index(a) for a in ("core", "yl", "yh"))
    so_core = (1 - 2 * core).astype(jnp.float32)
    so_y = (1 - 2 * yl).astype(jnp.float32)
    sgn_y, sgn = so_y[None], jnp.stack([so_core, so_y])
    core_at = core[None].astype(jnp.int32)
    idx = jnp.stack([core, 1 - core]).astype(jnp.int32)

    def of_mine(value):
        return lax.dynamic_slice_in_dim(value, core * half, half, 0)

    def of_part(value):
        return lax.dynamic_slice_in_dim(value, (1 - core) * half, half, 0)

    def diagonal(value):
        return xor(value, ("yl", "core"), 3)

    own = flip(idx, 0, hidden, sign_bits, half)
    part = flip(idx, 1, hidden, sign_bits, half, after=(own,))
    far, diag, near = swap(own, "yl"), diagonal(part), swap(part, "core")

    go_mine, go_part = of_mine(grad_out), of_part(grad_out)
    line = gather_z(after(go_mine, own))
    gq_here, gq_give = back(go_mine, go_part, down_weight, after=(own,))
    gq_there = swap(gq_give, "core")
    bound = 448.0 * jnp.exp2(exponents.astype(jnp.float32))
    bounds = (of_mine(bound), swap(of_part(bound), "core"))
    ring = after(line, far, gq_here)
    pieces = [ring, shift(ring, "x", 1), None, shift(ring, "x", 3)]

    q_here, q_there, qt, grads = turn(
        sgn, core_at, (own, near, far, diag), table, bounds, (gq_here, gq_there), norm, 64
    )
    got = lax.all_to_all(after(qt, pieces[1], pieces[3]), ("core", "z", "x"), 0, 0, tiled=True)
    v_here, v_there = turn_back(grads, table, half, ff_local, norm)
    pieces[2] = shift(after(ring, v_here), "x", 2)
    cross, dcross, ncross = swap(v_here, "yl"), diagonal(v_there), swap(v_there, "core")
    early = [swap(pieces[i], "core") for i in (0, 1, 3)]

    out_all = project((q_here, swap(q_there, "core")), down_weight, after=(v_here, *early)).reshape(2, 2, quarter, d_out)

    def share(y, c):
        tokens = lax.dynamic_index_in_dim(out_all, y ^ core, 0, keepdims=False)
        return lax.dynamic_index_in_dim(tokens, c, 0, keepdims=False)

    given = [swap(share(1 - yl, core), "yl"), swap(share(yl, 1 - core), "core"), diagonal(share(1 - yl, 1 - core))]
    grad_hidden = finish(idx, 0, sgn_y, v_here, cross, sign_bits)

    gated = after(pieces[2], out_all)
    quads = gated.shape[0] // 4
    late = [swap(gated[i * quads : (i + 1) * quads], "core") for i in range(4)]
    acc = weight_grad(source_places(), after(got, grad_hidden), pieces + [early[0], early[1], *late, early[2]], half)

    grad_hidden = finish(idx, 1, sgn_y, ncross, after(dcross, acc), sign_bits, into=grad_hidden)

    acc = acc.reshape(2, -1, d_out)
    keep = lax.dynamic_index_in_dim(acc, yh, 0, keepdims=False)
    give = lax.dynamic_index_in_dim(acc, 1 - yh, 0, keepdims=False).astype(jnp.bfloat16)
    taken = swap(give, "yh")
    grad_weight = (keep + taken.astype(jnp.float32)) * (1.0 / math.sqrt(tok_count * n_data))

    output = share(yl, core).astype(jnp.float32)
    for other in given:
        output = output + after(other, taken, grad_hidden).astype(jnp.float32)
    output = output.astype(jnp.bfloat16)
    return (output, grad_hidden, grad_weight)


def solution(mesh):
    fine = Mesh(mesh.devices.reshape(2, 8, 4, 2, 2), AXES)
    dp, tensor = ("yh", "z", "x"), ("yl", "core")
    return jax.shard_map(
        local,
        mesh=fine,
        in_specs=(P(dp, tensor), P(tensor), P(dp, tensor), P(tensor, None), P(dp, None)),
        out_specs=(P(dp + tensor, None), P(dp, tensor), P(tensor + dp, None)),
        check_vma=False,
    )
```
